32 devices in a mesh: section: 4 (over y, x), expert: 8 (over z, core).
Axes of the slice: x: 2, y: 2, z: 4, core: 2. Of those that a mesh axis runs over, the one named last changes fastest.
Arguments:
- tokens: bfloat16 [4096, 4096], P(('section', 'expert')), may hold values from -6 to 6
- expert_ids: int32 [4096], P(('section', 'expert')), may hold values from 0 to 7, as said below
- slot_ids: int32 [4096], P(('section', 'expert')), may hold values from 0 to 19, as said below
- router: bfloat16 [4096, 8], replicated, may hold values from -0.09375 to 0.09375
- w_in: bfloat16 [8, 4096, 5120], P('expert', None, 'section'), may hold values from -0.09375 to 0.09375
- w_out: bfloat16 [8, 5120, 4096], P('expert', 'section'), may hold values from -0.078125 to 0.078125
Outputs:
- moe_out: bfloat16 [4096, 4096], P(('section', 'expert'))
The draws below stay inside these ranges and needn't reach their ends.
Inputs may be any that keep to these rules, and one draw needn't show every extreme that they name: `expert_ids`: within each aligned block of 128 rows (the tokens of one device) no pair of expert id and slot position occurs twice, so each expert receives at most 20 tokens from one device. `slot_ids`: a token's position among the 20 slots that its device keeps for its expert.
All inputs are finite; a program needn't handle non-finite values.
Results may differ from the reference program's by a relative error of at most 0.018.
Values may be sent and summed in bfloat16 or wider, within the bound.
A program may use at most 128 MiB of HBM per device.

```python
import jax
import jax.numpy as jnp
from jax import lax

D = 4096
FF = 5120
TOK_DEV = 128
EXPERTS = 8
CAP = 20
TOKENS = 4096
N_SECTION = 4


def routing_cells(key):
    base_key = jax.random.fold_in(key, 11)
    block_count = TOKENS // TOK_DEV
    cell_count = EXPERTS * CAP
    full_expert = jax.random.randint(jax.random.fold_in(base_key, 3), (), 0, EXPERTS)

    def draw_block(block_index):
        block_key = jax.random.fold_in(base_key, block_index + 100)
        score_key, order_key = jax.random.split(block_key)
        scores = jax.random.randint(score_key, (cell_count,), 0, 65536) * cell_count + jnp.arange(cell_count, dtype=jnp.int32)
        owners = jnp.arange(cell_count, dtype=jnp.int32) // CAP
        scores = jnp.where(owners == full_expert, scores + 268435456, scores)
        taken = lax.top_k(scores, TOK_DEV)[1]
        return jax.random.permutation(order_key, taken)
    chosen = jax.vmap(draw_block)(jnp.arange(block_count, dtype=jnp.int32))
    return chosen.reshape(-1).astype(jnp.int32)


def draw_expert_ids(key, part):
    return (routing_cells(key) // CAP).astype(jnp.int32)


def draw_slot_ids(key, part):
    return (routing_cells(key) % CAP).astype(jnp.int32)


def block_levels(stream_key, extent, cuts, least, largest):
    gain = 1.0
    for dim, parts in cuts:
        heights = jax.random.uniform(jax.random.fold_in(jax.random.fold_in(stream_key, 6), dim), (parts,), jnp.float32, least / len(cuts), largest / len(cuts))
        gain = gain * jnp.repeat(jnp.exp(heights), extent[dim] // parts).reshape((-1,) + (1,) * (len(extent) - 1 - dim))
    return gain


def bell_draw(own_key, extent, deviation, most, shards=(), kind=jnp.bfloat16):
    drawn = jax.random.normal(own_key, extent, jnp.float32) * deviation
    if len(shards) > 0:
        drawn = block_levels(own_key, extent, shards, -0.22, 0.18) * drawn
    return jnp.clip(drawn, min=-most, max=most).astype(kind)


def setup_inputs(seed: int = 0) -> dict:
    seeds = jax.random.split(jax.random.key(seed), 7)
    return {
        "tokens": bell_draw(seeds[0], (TOKENS, D), 1.0, 6.0, ((0, 32),)),
        "expert_ids": draw_expert_ids(jax.random.fold_in(seeds[6], 71), 0),
        "slot_ids": draw_slot_ids(jax.random.fold_in(seeds[6], 71), 0),
        "router": bell_draw(seeds[3], (D, EXPERTS), D ** -0.5, 0.09375),
        "w_in": bell_draw(seeds[4], (EXPERTS, D, FF), D ** -0.5, 0.09375, ((0, 8), (2, 4))),
        "w_out": bell_draw(seeds[5], (EXPERTS, FF, D), FF ** -0.5, 0.078125, ((0, 8), (1, 4))),
    }


def reference(tokens, expert_ids, slot_ids, router, w_in, w_out):
    tok_total = tokens.shape[0]
    block_count = tok_total // TOK_DEV
    group_width = FF // N_SECTION
    logits = jnp.dot(tokens, router, preferred_element_type=jnp.float32)
    chosen = expert_ids[:, None] == jnp.arange(EXPERTS, dtype=jnp.int32)[None, :]
    gating = jax.nn.sigmoid(jnp.sum(jnp.where(chosen, logits, jnp.zeros_like(logits)), axis=1))
    block_of = (jnp.arange(tok_total, dtype=jnp.int32) // TOK_DEV).astype(jnp.int32)
    position = ((expert_ids * block_count + block_of) * CAP + slot_ids).astype(jnp.int32)
    slot_table = jnp.zeros((EXPERTS * block_count * CAP, D), jnp.bfloat16).at[position].set(tokens)
    slot_table = slot_table.reshape(EXPERTS, block_count * CAP, D)

    def expert_ffn(operands):
        slot_rows, inward, outward = operands
        hidden = jax.nn.relu(jnp.dot(slot_rows, inward, preferred_element_type=jnp.float32)).astype(jnp.bfloat16)
        hidden = lax.optimization_barrier(hidden)
        grouped = hidden.reshape(slot_rows.shape[0], N_SECTION, group_width).astype(jnp.float32)
        out_groups = outward.reshape(N_SECTION, group_width, D).astype(jnp.float32)
        partial_value = jnp.einsum("rgf,gfd->grd", grouped, out_groups).astype(jnp.bfloat16)
        partial_value = lax.optimization_barrier(partial_value)
        return jnp.sum(partial_value.astype(jnp.float32), axis=0).astype(jnp.bfloat16)

    expert_out = lax.map(expert_ffn, (slot_table, w_in, w_out))
    picked = expert_out.reshape(-1, D)[position]
    return (gating[:, None] * picked.astype(jnp.float32)).astype(jnp.bfloat16)
```

```python
import functools
import math

import jax
import jax.numpy as jnp
from jax import lax
from jax.experimental import pallas as pl
from jax.experimental.pallas import tpu as pltpu
from jax.sharding import PartitionSpec as P

MESH = pl.DeviceIdType.MESH
BF16 = jnp.bfloat16
F32 = jnp.float32
CHUNKS = 8


def per_device(tokens, expert_ids, slot_ids, router, w_in, w_out):
    tok_rows, width_model = tokens.shape
    experts = router.shape[1]
    capacity = 5 * tok_rows // (4 * experts)
    cell_index = expert_ids * capacity + slot_ids
    onehot = (
        cell_index[None, :] == jnp.arange(experts * capacity, dtype=jnp.int32)[:, None]
    ).astype(jnp.bfloat16)
    dispatch = jnp.dot(onehot, tokens, preferred_element_type=jnp.float32).astype(jnp.bfloat16)
    dispatch = dispatch.reshape(experts, capacity, width_model)
    inward = w_in[0]
    outward = w_out[0]
    arrived = lax.all_to_all(dispatch, "expert", split_axis=0, concat_axis=0, tiled=True)
    flat = lax.all_gather(arrived.reshape(-1, width_model), "section", axis=0, tiled=True)
    hidden = jax.nn.relu(jnp.dot(flat, inward, preferred_element_type=jnp.float32)).astype(
        jnp.bfloat16
    )
    summed = lax.psum_scatter(
        jnp.dot(hidden, outward, preferred_element_type=jnp.float32).astype(jnp.bfloat16),
        "section",
        scatter_dimension=0,
        tiled=True,
    )
    expert_out = summed.reshape(experts, capacity, width_model)
    returned = lax.all_to_all(expert_out, "expert", split_axis=0, concat_axis=0, tiled=True)
    combined = lax.dot_general(
        onehot,
        returned.reshape(-1, width_model),
        (((0,), (0,)), ((), ())),
        preferred_element_type=jnp.float32,
    )
    logits = jnp.dot(tokens, router, preferred_element_type=jnp.float32)
    chosen = expert_ids[:, None] == jnp.arange(experts, dtype=jnp.int32)[None, :]
    gating = jax.nn.sigmoid(jnp.sum(jnp.where(chosen, logits, jnp.zeros_like(logits)), axis=1))
    return (gating[:, None] * combined).astype(jnp.bfloat16)


def divide(value, number):
    return lax.shift_right_logical(value * (-(-(1 << 20) // number)), 20)


def iota(shape, dim):
    return lax.broadcasted_iota(jnp.int32, shape, dim)


def one_where(condition):
    return jnp.where(condition, 1.0, 0.0).astype(BF16)


def dot(a, b):
    return jnp.dot(a, b, preferred_element_type=F32)


def kernel(
    dims, tok, eid, sid, router, w_in, w_out, out,
    disp, arr, xall, acc, hid, win, wout, part, half, fin, back, ret,
    d_mat, p_mat, pt_mat, c_mat, gate,
    win_sem, wout_sem, d_send, d_recv, g_send, g_recv, s_send, s_recv, b_send, b_recv,
):
    E, C, Q, G, W, S, T, H = dims
    B, R = Q * C, E * C
    h = R // 2
    section, expert = lax.axis_index("section"), lax.axis_index("expert")
    y, x = section // 2, section % 2
    xn = {"section": y * 2 + (1 - x), "expert": expert}
    yn = {"section": (1 - y) * 2 + x, "expert": expert}
    peers = [(expert + d) % E for d in range(1, E)]

    def in_copy(c):
        return pltpu.make_async_copy(w_in.at[0, pl.ds(c * W, W)], win.at[c], win_sem.at[c])

    def out_copy(c):
        columns = pl.ds(pl.multiple_of(c * W, W), W)
        return pltpu.make_async_copy(w_out.at[0, :, columns], wout.at[c], wout_sem.at[c])

    def exchange_start(src, dst, send, recv, c):
        mine = pl.ds(expert * B, B)
        for p in peers:
            pltpu.make_async_remote_copy(
                src_ref=src.at[c, pl.ds(p * B, B)],
                dst_ref=dst.at[c, mine],
                send_sem=send.at[c],
                recv_sem=recv.at[c],
                device_id={"section": section, "expert": p},
                device_id_type=MESH,
            ).start()
        pltpu.make_async_copy(src.at[c, mine], dst.at[c, mine], recv.at[c]).start()

    def exchange_arrived(dst, recv, c):
        pltpu.make_async_copy(dst.at[c], dst.at[c], recv.at[c]).wait()

    def exchange_sent(src, send, c):
        others = src.at[c, pl.ds(0, (E - 1) * B)]
        pltpu.make_async_copy(others, others, send.at[c]).wait()

    def hop(src, src_row, dst, dst_row, rows, send, recv, index, c, target):
        return pltpu.make_async_remote_copy(
            src_ref=src.at[c, pl.ds(src_row, rows)],
            dst_ref=dst.at[c, pl.ds(dst_row, rows)],
            send_sem=send.at[index, c],
            recv_sem=recv.at[index, c],
            device_id=target,
            device_id_type=MESH,
        )

    def gather_hop(index, c):
        src_row, dst_row, rows, target = (
            (0, R, R, xn),
            (0, 2 * R, R, yn),
            (R, 3 * R, h, yn),
            (2 * R + h, 3 * R + h, h, xn),
        )[index]
        return hop(xall, src_row, xall, dst_row, rows, g_send, g_recv, index, c, target)

    def scatter_hop(index, c):
        src_row, dst, dst_row, target = (
            (3 * R, half, 0, xn),
            (3 * R + h, half, h, yn),
            (R, fin, 0, xn),
            (2 * R + h, fin, R + h, yn),
            (R + h, fin, h, xn),
            (2 * R, fin, R, yn),
        )[index]
        return hop(part, src_row, dst, dst_row, h, s_send, s_recv, index, c, target)

    barrier = pltpu.get_barrier_semaphore()
    for p in peers:
        pl.semaphore_signal(
            barrier, inc=1, device_id={"section": section, "expert": p}, device_id_type=MESH
        )
    for target in (xn, yn):
        pl.semaphore_signal(barrier, inc=1, device_id=target, device_id_type=MESH)

    def keys(shape, dim):
        r = iota(shape, dim)
        block = divide(r, B)
        inner = r - block * B
        quarter = divide(inner, C)
        return quarter * R + block * C + (inner - quarter * C)

    cell_row = eid[...] * C + sid[...]
    diagonal = iota((T, T), 0) == iota((T, T), 1)
    column = lambda row: jnp.sum(
        jnp.where(diagonal, jnp.broadcast_to(row, (T, T)), 0).astype(F32), axis=1, keepdims=True
    ).astype(jnp.int32)

    key = keys((E * B, T), 0)
    for q in range(Q):
        d_mat[q] = one_where(key == cell_row + q * R)

    def dispatch(c):
        total = None
        for q in range(Q):
            columns = pl.ds(pl.multiple_of(c * W + q * S, S), S)
            term = dot(d_mat[q], tok[:, columns])
            total = term if total is None else total + term
        disp[c] = total.astype(BF16)

    dispatch(0)
    pl.semaphore_wait(barrier, E + 1)
    exchange_start(disp, arr, d_send, d_recv, 0)

    @pl.loop(0, G)
    def _(c):
        in_copy(c).start()

    key = keys((R, E * B), 1)
    for q in range(Q):
        p_mat[q] = one_where(key == iota((R, E * B), 0) + q * R)

    @pl.loop(0, G + 2)
    def _(c):
        @pl.when(c + 1 < G)
        def _():
            dispatch(c + 1)
            exchange_start(disp, arr, d_send, d_recv, c + 1)

        @pl.when(c < G)
        def _():
            out_copy(c).start()
            exchange_arrived(arr, d_recv, c)
            for q in range(Q):
                xall[c, 0:R, q * S : (q + 1) * S] = dot(p_mat[q], arr[c]).astype(BF16)
            gather_hop(0, c).start()
            gather_hop(1, c).start()

        @pl.when(c == 0)
        def _():
            key = keys((E * B, R), 0)
            for q in range(Q):
                pt_mat[q] = one_where(key == iota((E * B, R), 1) + q * R)
            key = keys((T, E * B), 1)
            cell_column = column(cell_row)
            for q in range(Q):
                c_mat[q] = one_where(key == cell_column + q * R)
            logits = dot(tok[...], router[...])
            chosen = column(eid[...]) == iota((T, E), 1)
            picked = jnp.sum(jnp.where(chosen, logits, 0.0), axis=1, keepdims=True)
            gate[...] = 1.0 / (1.0 + jnp.exp(-picked))
            acc[...] = jnp.zeros_like(acc)

        @pl.when((c >= 1) & (c <= G))
        def _():
            k = c - 1
            gather_hop(0, k).wait_recv()
            gather_hop(2, k).start()
            gather_hop(1, k).wait_recv()
            gather_hop(3, k).start()

        @pl.when(c >= 2)
        def _():
            k = c - 2
            gather_hop(2, k).wait_recv()
            gather_hop(3, k).wait_recv()
            in_copy(k).wait()

            @pl.loop(0, H // 256)
            def _(n):
                columns = pl.ds(pl.multiple_of(n * 256, 256), 256)
                acc[:, columns] += dot(xall[k], win[k, :, columns])

    @pl.loop(0, H // 256)
    def _(n):
        columns = pl.ds(pl.multiple_of(n * 256, 256), 256)
        hid[:, columns] = jnp.maximum(acc[:, columns], 0.0).astype(BF16)

    @pl.loop(0, G + 3)
    def _(c):
        @pl.when(c < G)
        def _():
            out_copy(c).wait()

            @pl.loop(0, W // 256)
            def _(n):
                columns = pl.ds(pl.multiple_of(n * 256, 256), 256)
                part[c, :, columns] = dot(hid[...], wout[c, :, columns]).astype(BF16)

            for index in range(4):
                scatter_hop(index, c).start()

        @pl.when((c >= 1) & (c <= G))
        def _():
            k = c - 1
            scatter_hop(0, k).wait_recv()
            part[k, 2 * R : 2 * R + h] = (
                part[k, 2 * R : 2 * R + h].astype(F32) + half[k, 0:h].astype(F32)
            ).astype(BF16)
            scatter_hop(5, k).start()
            scatter_hop(1, k).wait_recv()
            part[k, R + h : 2 * R] = (
                part[k, R + h : 2 * R].astype(F32) + half[k, h:R].astype(F32)
            ).astype(BF16)
            scatter_hop(4, k).start()

        @pl.when((c >= 2) & (c <= G + 1))
        def _():
            k = c - 2
            for index in range(2, 6):
                scatter_hop(index, k).wait_recv()
            summed = (
                part[k, 0:R].astype(F32) + fin[k, 0:R].astype(F32) + fin[k, R : 2 * R].astype(F32)
            ).astype(BF16)
            total = None
            for q in range(Q):
                term = dot(pt_mat[q], summed[:, q * S : (q + 1) * S])
                total = term if total is None else total + term
            back[k] = total.astype(BF16)
            exchange_start(back, ret, b_send, b_recv, k)

        @pl.when(c >= 3)
        def _():
            k = c - 3
            exchange_arrived(ret, b_recv, k)
            for q in range(Q):
                columns = pl.ds(pl.multiple_of(k * W + q * S, S), S)
                out[:, columns] = (gate[...] * dot(c_mat[q], ret[k])).astype(BF16)

    @pl.loop(0, G)
    def _(c):
        exchange_sent(disp, d_send, c)
        exchange_sent(back, b_send, c)
        for index in range(4):
            gather_hop(index, c).wait_send()
        for index in range(6):
            scatter_hop(index, c).wait_send()


def fused(tokens, expert_ids, slot_ids, router, w_in, w_out):
    T, D = tokens.shape
    E = router.shape[1]
    C = 5 * T // (4 * E)
    H = w_in.shape[2]
    Q = 16 // math.gcd(16, C)
    G = min(CHUNKS, D // (128 * Q))
    W = D // G
    S = W // Q
    B, R = Q * C, E * C
    dims = (E, C, Q, G, W, S, T, H)
    vmem = pl.BlockSpec(memory_space=pltpu.VMEM)
    hbm = pl.BlockSpec(memory_space=pl.ANY)
    dma = pltpu.SemaphoreType.DMA
    return pl.pallas_call(
        functools.partial(kernel, dims),
        out_shape=jax.ShapeDtypeStruct((T, D), BF16),
        in_specs=[vmem, vmem, vmem, vmem, hbm, hbm],
        out_specs=vmem,
        scratch_shapes=[
            pltpu.VMEM((G, E * B, S), BF16),
            pltpu.VMEM((G, E * B, S), BF16),
            pltpu.VMEM((G, 4 * R, W), BF16),
            pltpu.VMEM((4 * R, H), F32),
            pltpu.VMEM((4 * R, H), BF16),
            pltpu.VMEM((G, W, H), BF16),
            pltpu.VMEM((G, H, W), BF16),
            pltpu.VMEM((G, 4 * R, W), BF16),
            pltpu.VMEM((G, R, W), BF16),
            pltpu.VMEM((G, 2 * R, W), BF16),
            pltpu.VMEM((G, E * B, S), BF16),
            pltpu.VMEM((G, E * B, S), BF16),
            pltpu.VMEM((Q, E * B, T), BF16),
            pltpu.VMEM((Q, R, E * B), BF16),
            pltpu.VMEM((Q, E * B, R), BF16),
            pltpu.VMEM((Q, T, E * B), BF16),
            pltpu.VMEM((T, 1), F32),
            dma((G,)), dma((G,)), dma((G,)), dma((G,)),
            dma((4, G)), dma((4, G)), dma((6, G)), dma((6, G)),
            dma((G,)), dma((G,)),
        ],
        compiler_params=pltpu.CompilerParams(
            collective_id=0, has_side_effects=True, vmem_limit_bytes=62 * 1024 * 1024
        ),
        cost_estimate=pl.CostEstimate(
            flops=16 * R * D * H, bytes_accessed=4 * D * H, transcendentals=T
        ),
    )(tokens, expert_ids.reshape(1, T), slot_ids.reshape(1, T), router, w_in, w_out)


def solution(mesh):
    body = fused if mesh.shape["section"] == 4 else per_device
    return jax.shard_map(
        body,
        mesh=mesh,
        in_specs=(
            P(("section", "expert"), None),
            P(("section", "expert")),
            P(("section", "expert")),
            P(),
            P("expert", None, "section"),
            P("expert", "section", None),
        ),
        out_specs=P(("section", "expert"), None),
        check_vma=False,
    )
```

```python
import functools
import math

import jax
import jax.numpy as jnp
from jax import lax
from jax.experimental import pallas as pl
from jax.experimental.pallas import tpu as pltpu
from jax.sharding import PartitionSpec as P

MESH = pl.DeviceIdType.MESH
BF16 = jnp.bfloat16
F32 = jnp.float32
CHUNKS = 8


def per_device(tokens, expert_ids, slot_ids, router, w_in, w_out):
    tok_rows, width_model = tokens.shape
    experts = router.shape[1]
    capacity = 5 * tok_rows // (4 * experts)
    cell_index = expert_ids * capacity + slot_ids
    onehot = (
        cell_index[None, :] == jnp.arange(experts * capacity, dtype=jnp.int32)[:, None]
    ).astype(jnp.bfloat16)
    dispatch = jnp.dot(onehot, tokens, preferred_element_type=jnp.float32).astype(jnp.bfloat16)
    dispatch = dispatch.reshape(experts, capacity, width_model)
    inward = w_in[0]
    outward = w_out[0]
    arrived = lax.all_to_all(dispatch, "expert", split_axis=0, concat_axis=0, tiled=True)
    flat = lax.all_gather(arrived.reshape(-1, width_model), "section", axis=0, tiled=True)
    hidden = jax.nn.relu(jnp.dot(flat, inward, preferred_element_type=jnp.float32)).astype(
        jnp.bfloat16
    )
    summed = lax.psum_scatter(
        jnp.dot(hidden, outward, preferred_element_type=jnp.float32).astype(jnp.bfloat16),
        "section",
        scatter_dimension=0,
        tiled=True,
    )
    expert_out = summed.reshape(experts, capacity, width_model)
    returned = lax.all_to_all(expert_out, "expert", split_axis=0, concat_axis=0, tiled=True)
    combined = lax.dot_general(
        onehot,
        returned.reshape(-1, width_model),
        (((0,), (0,)), ((), ())),
        preferred_element_type=jnp.float32,
    )
    logits = jnp.dot(tokens, router, preferred_element_type=jnp.float32)
    chosen = expert_ids[:, None] == jnp.arange(experts, dtype=jnp.int32)[None, :]
    gating = jax.nn.sigmoid(jnp.sum(jnp.where(chosen, logits, jnp.zeros_like(logits)), axis=1))
    return (gating[:, None] * combined).astype(jnp.bfloat16)


def divide(value, number):
    return lax.shift_right_logical(value * (-(-(1 << 20) // number)), 20)


def iota(shape, dim):
    return lax.broadcasted_iota(jnp.int32, shape, dim)


def one_where(condition):
    return jnp.where(condition, 1.0, 0.0).astype(BF16)


def dot(a, b):
    return jnp.dot(a, b, preferred_element_type=F32)


def kernel(
    dims, tok, eid, sid, router, w_in, w_out, out,
    near_disp, far_disp, near_x, far_x, x_chunk, acc, hid, win, wout, p_chunk,
    near_part, far_part, near_half, far_half, near_fin, far_fin,
    near_back, far_back, near_ret, far_ret,
    d_mat, p_mat, pt_mat, c_mat, gate, comb, out_v,
    win_sem, wout_sem, out_sem,
    near_d_send, near_d_recv, far_d_send, far_d_recv,
    near_g_send, near_g_recv, far_g_send, far_g_recv,
    near_s_send, near_s_recv, far_s_send, far_s_recv,
    near_b_send, near_b_recv, far_b_send, far_b_recv,
):
    E, C, Q, G, U, W, S, T, H = dims
    B, R = Q * C, E * C
    V = G // U
    NEAR, FAR = 2 * V * B, (E - 2) * B
    section, expert = lax.axis_index("section"), lax.axis_index("expert")
    y, x = section // 2, section % 2
    core = expert % 2
    chip = expert - core
    xn = {"section": y * 2 + (1 - x), "expert": expert}
    yn = {"section": (1 - y) * 2 + x, "expert": expert}
    sibling = {"section": section, "expert": chip + 1 - core}
    far = [({"section": section, "expert": (chip + d) % E}, d) for d in range(2, E)]

    def in_copy(c):
        return pltpu.make_async_copy(w_in.at[0, pl.ds(c * W, W)], win.at[c], win_sem.at[c])

    def out_copy(c):
        columns = pl.ds(pl.multiple_of(c * W, W), W)
        return pltpu.make_async_copy(w_out.at[0, :, columns], wout.at[c], wout_sem.at[c])

    def result_copy(u):
        columns = pl.ds(pl.multiple_of(u * V * W, V * W), V * W)
        return pltpu.make_async_copy(out_v.at[:, columns], out.at[:, columns], out_sem.at[u])

    def far_start(src, dst, send, recv, c):
        for target, d in far:
            row = pl.multiple_of((core + E - 2 * (d // 2) - 2) * B, 16)
            pltpu.make_async_remote_copy(
                src_ref=src.at[c, pl.ds((d - 2) * B, B)],
                dst_ref=dst.at[c, pl.ds(row, B)],
                send_sem=send.at[c],
                recv_sem=recv.at[c],
                device_id=target,
                device_id_type=MESH,
            ).start()

    def near_start(src, dst, send, recv, u):
        mine = pl.ds(pl.multiple_of(core * (V * B), 16), V * B)
        other = pl.ds(pl.multiple_of((1 - core) * (V * B), 16), V * B)
        pltpu.make_async_remote_copy(
            src_ref=src.at[u, other],
            dst_ref=dst.at[u, mine],
            send_sem=send.at[u],
            recv_sem=recv.at[u],
            device_id=sibling,
            device_id_type=MESH,
        ).start()
        pltpu.make_async_copy(src.at[u, mine], dst.at[u, mine], recv.at[u]).start()

    def await_rows(ref, sem, index, rows):
        view = ref.at[index, pl.ds(0, rows)]
        pltpu.make_async_copy(view, view, sem.at[index]).wait()

    def hop(src, src_row, dst, dst_row, rows, send, recv, index, c, target):
        return pltpu.make_async_remote_copy(
            src_ref=src.at[c, pl.ds(src_row, rows)],
            dst_ref=dst.at[c, pl.ds(dst_row, rows)],
            send_sem=send.at[index, c],
            recv_sem=recv.at[index, c],
            device_id=target,
            device_id_type=MESH,
        )

    def gather_hop(buffers, index, c):
        held, n, send, recv = buffers
        h = n // 2
        src_row, dst_row, rows, target = (
            (0, n, n, xn),
            (0, 2 * n, n, yn),
            (n, 3 * n, h, yn),
            (2 * n + h, 3 * n + h, h, xn),
        )[index]
        return hop(held, src_row, held, dst_row, rows, send, recv, index, c, target)

    def scatter_hop(buffers, index, c):
        part, half, fin, n, send, recv = buffers
        h = n // 2
        src_row, dst, dst_row, target = (
            (3 * n, half, 0, xn),
            (3 * n + h, half, h, yn),
            (n, fin, 0, xn),
            (2 * n + h, fin, n + h, yn),
            (n + h, fin, h, xn),
            (2 * n, fin, n, yn),
        )[index]
        return hop(part, src_row, dst, dst_row, h, send, recv, index, c, target)

    near_g = (near_x, NEAR, near_g_send, near_g_recv)
    far_g = (far_x, FAR, far_g_send, far_g_recv)
    near_s = (near_part, near_half, near_fin, NEAR, near_s_send, near_s_recv)
    far_s = (far_part, far_half, far_fin, FAR, far_s_send, far_s_recv)

    def gather_own(buffers, c):
        gather_hop(buffers, 0, c).start()
        gather_hop(buffers, 1, c).start()

    def gather_relay(buffers, c):
        gather_hop(buffers, 0, c).wait_recv()
        gather_hop(buffers, 2, c).start()
        gather_hop(buffers, 1, c).wait_recv()
        gather_hop(buffers, 3, c).start()

    def gather_rest(buffers, c):
        gather_hop(buffers, 2, c).wait_recv()
        gather_hop(buffers, 3, c).wait_recv()

    def scatter_own(buffers, c):
        for index in range(4):
            scatter_hop(buffers, index, c).start()

    def scatter_relay(buffers, c):
        part, half, _, n, _, _ = buffers
        h = n // 2
        for wait, row, at, send in ((0, 2 * n, 0, 5), (1, n + h, h, 4)):
            scatter_hop(buffers, wait, c).wait_recv()
            part[c, row : row + h] = (
                part[c, row : row + h].astype(F32) + half[c, at : at + h].astype(F32)
            ).astype(BF16)
            scatter_hop(buffers, send, c).start()

    def scatter_total(buffers, c, back):
        part, _, fin, n, _, _ = buffers
        for index in range(2, 6):
            scatter_hop(buffers, index, c).wait_recv()
        back[c] = (
            part[c, 0:n].astype(F32) + fin[c, 0:n].astype(F32) + fin[c, n : 2 * n].astype(F32)
        ).astype(BF16)

    barrier = pltpu.get_barrier_semaphore()
    for target in [target for target, _ in far] + [sibling, xn, yn]:
        pl.semaphore_signal(barrier, inc=1, device_id=target, device_id_type=MESH)

    def keys(shape, dim, first):
        r = iota(shape, dim)
        block = divide(r, B)
        inner = r - block * B
        quarter = divide(inner, C)
        owner = block + first
        owner = jnp.where(owner >= E, owner - E, owner)
        return quarter * R + owner * C + (inner - quarter * C)

    cell_row = eid[...] * C + sid[...]
    diagonal = iota((T, T), 0) == iota((T, T), 1)

    def column(row):
        spread = jnp.where(diagonal, jnp.broadcast_to(row, (T, T)), 0).astype(F32)
        return jnp.sum(spread, axis=1, keepdims=True).astype(jnp.int32)

    key = keys((E * B, T), 0, chip)
    for q in range(Q):
        d_mat[:, q * T : (q + 1) * T] = one_where(key == cell_row + q * R)

    def stacked(c):
        return jnp.concatenate(
            [tok[:, pl.ds(pl.multiple_of(c * W + q * S, S), S)] for q in range(Q)], axis=0
        )

    def far_dispatch(c):
        far_disp[c] = dot(d_mat[2 * B :], stacked(c)).astype(BF16)
        far_start(far_disp, far_x, far_d_send, far_d_recv, c)

    for u in range(U):
        for v in range(V):
            rows = dot(d_mat[0 : 2 * B], stacked(u * V + v)).astype(BF16)
            near_disp[u, v * B : (v + 1) * B] = rows[0:B]
            near_disp[u, (V + v) * B : (V + v + 1) * B] = rows[B : 2 * B]
    pl.semaphore_wait(barrier, E + 1)
    for u in range(U):
        near_start(near_disp, near_x, near_d_send, near_d_recv, u)
    far_dispatch(0)
    for u in range(U):
        await_rows(near_x, near_d_recv, u, NEAR)
        gather_own(near_g, u)
    far_dispatch(1)

    @pl.loop(0, G)
    def _(c):
        in_copy(c).start()

    key = keys((R * Q, E * B), 1, 0)
    p_mat[...] = one_where(key == iota((R * Q, E * B), 0))
    acc[...] = jnp.zeros_like(acc)

    def near_rows(ref, k, base):
        u, v = k // V, k % V
        first = pl.multiple_of(base + v * B, 16)
        second = pl.multiple_of(base + (V + v) * B, 16)
        return [ref[u, pl.ds(first, B)], ref[u, pl.ds(second, B)]]

    @pl.loop(0, G + 3)
    def _(c):
        @pl.when(c + 2 < G)
        def _():
            far_dispatch(c + 2)

        @pl.when(c < G)
        def _():
            out_copy(c).start()
            await_rows(far_x, far_d_recv, c, FAR)
            gather_own(far_g, c)

        @pl.when(c < U)
        def _():
            gather_relay(near_g, c)

        @pl.when(c == 0)
        def _():
            key = keys((E * B, R * Q), 0, 0)
            pt_mat[...] = one_where(key == iota((E * B, R * Q), 1))
            key = keys((T, E * B), 1, chip)
            cell_column = column(cell_row)
            for q in range(Q):
                c_mat[q * T : (q + 1) * T] = one_where(key == cell_column + q * R)
            logits = lax.dot_general(
                tok[...], router[...], (((1,), (1,)), ((), ())), preferred_element_type=F32
            )
            chosen = column(eid[...]) == iota((T, E), 1)
            picked = jnp.sum(jnp.where(chosen, logits, 0.0), axis=1, keepdims=True)
            gate[...] = 1.0 / (1.0 + jnp.exp(-picked))

        @pl.when((c >= 2) & (c < G + 2))
        def _():
            gather_relay(far_g, c - 2)

        @pl.when(c == 2)
        def _():
            for u in range(U):
                gather_rest(near_g, u)

        @pl.when(c >= 3)
        def _():
            k = c - 3
            gather_rest(far_g, k)
            raw = [
                jnp.concatenate(
                    near_rows(near_x, k, s * NEAR) + [far_x[k, s * FAR : (s + 1) * FAR]], axis=0
                )
                for s in range(4)
            ]
            moved = dot(p_mat[...], jnp.concatenate(raw, axis=1)).astype(BF16)
            for s in range(4):
                for q in range(Q):
                    x_chunk[s * R : (s + 1) * R, q * S : (q + 1) * S] = moved[
                        q * R : (q + 1) * R, s * S : (s + 1) * S
                    ]
            in_copy(k).wait()

            @pl.loop(0, H // 256)
            def _(n):
                columns = pl.ds(pl.multiple_of(n * 256, 256), 256)
                acc[:, columns] += dot(x_chunk[...], win[k, :, columns])

    @pl.loop(0, H // 256)
    def _(n):
        columns = pl.ds(pl.multiple_of(n * 256, 256), 256)
        hid[:, columns] = jnp.maximum(acc[:, columns], 0.0).astype(BF16)

    def combine_near(u):
        await_rows(near_ret, near_b_recv, u, NEAR)
        for v in range(V):
            rows = jnp.concatenate(near_rows(near_ret, u * V + v, 0), axis=0)
            term = dot(c_mat[:, 0 : 2 * B], rows)
            for q in range(Q):
                at = (u * V + v) * W + q * S
                out_v[:, at : at + S] = (
                    gate[...] * (comb[:, at : at + S] + term[q * T : (q + 1) * T])
                ).astype(BF16)
        result_copy(u).start()

    def when_unit(index, near_step, far_step):
        @pl.when((index >= 0) & (index < G))
        def _():
            far_step(index)

        @pl.when((index >= G) & (index < G + U))
        def _():
            near_step(index - G)

    def far_own(c):
        out_copy(c).wait()

        @pl.loop(0, W // 256)
        def _(n):
            columns = pl.ds(pl.multiple_of(n * 256, 256), 256)
            p_chunk[:, columns] = dot(hid[...], wout[c, :, columns]).astype(BF16)

        rows = [
            jnp.concatenate(
                [p_chunk[s * R : (s + 1) * R, q * S : (q + 1) * S] for s in range(4)], axis=1
            )
            for q in range(Q)
        ]
        moved = dot(pt_mat[...], jnp.concatenate(rows, axis=0)).astype(BF16)
        u, v = c // V, c % V
        for s in range(4):
            columns = slice(s * S, (s + 1) * S)
            far_part[c, s * FAR : (s + 1) * FAR] = moved[2 * B :, columns]
            first = pl.multiple_of(s * NEAR + v * B, 16)
            second = pl.multiple_of(s * NEAR + (V + v) * B, 16)
            near_part[u, pl.ds(first, B)] = moved[0:B, columns]
            near_part[u, pl.ds(second, B)] = moved[B : 2 * B, columns]
        scatter_own(far_s, c)

    def far_total(c):
        scatter_total(far_s, c, far_back)
        far_start(far_back, far_ret, far_b_send, far_b_recv, c)

    def near_total(u):
        scatter_total(near_s, u, near_back)
        near_start(near_back, near_ret, near_b_send, near_b_recv, u)

    def far_combine(c):
        await_rows(far_ret, far_b_recv, c, FAR)
        term = dot(c_mat[:, 2 * B :], far_ret[c])
        for q in range(Q):
            columns = pl.ds(pl.multiple_of(c * W + q * S, S), S)
            comb[:, columns] = term[q * T : (q + 1) * T]

    @pl.loop(0, G + U + 3)
    def _(c):
        when_unit(c, lambda u: scatter_own(near_s, u), far_own)
        when_unit(
            c - 2, lambda u: scatter_relay(near_s, u), lambda k: scatter_relay(far_s, k)
        )
        when_unit(c - 3, near_total, far_total)

        @pl.when(c >= U + 3)
        def _():
            far_combine(c - U - 3)

    for u in range(U):
        combine_near(u)

    @pl.loop(0, G)
    def _(c):
        await_rows(far_disp, far_d_send, c, FAR)
        await_rows(far_back, far_b_send, c, FAR)
        for index in range(4):
            gather_hop(far_g, index, c).wait_send()
        for index in range(6):
            scatter_hop(far_s, index, c).wait_send()

    for u in range(U):
        await_rows(near_disp, near_d_send, u, V * B)
        await_rows(near_back, near_b_send, u, V * B)
        for index in range(4):
            gather_hop(near_g, index, u).wait_send()
        for index in range(6):
            scatter_hop(near_s, index, u).wait_send()
        result_copy(u).wait()


def fused(tokens, expert_ids, slot_ids, router, w_in, w_out):
    T, D = tokens.shape
    E = router.shape[1]
    C = 5 * T // (4 * E)
    H = w_in.shape[2]
    Q = 16 // math.gcd(16, C)
    G = min(CHUNKS, D // (128 * Q))
    U = 2
    W = D // G
    S = W // Q
    B, R = Q * C, E * C
    NEAR, FAR = 2 * (G // U) * B, (E - 2) * B
    dims = (E, C, Q, G, U, W, S, T, H)
    vmem = pl.BlockSpec(memory_space=pltpu.VMEM)
    hbm = pl.BlockSpec(memory_space=pl.ANY)
    dma = pltpu.SemaphoreType.DMA
    rows = lambda near, far: [pltpu.VMEM((U, near, S), BF16), pltpu.VMEM((G, far, S), BF16)]
    return pl.pallas_call(
        functools.partial(kernel, dims),
        out_shape=jax.ShapeDtypeStruct((T, D), BF16),
        in_specs=[vmem, vmem, vmem, vmem, hbm, hbm],
        out_specs=hbm,
        scratch_shapes=rows(NEAR, FAR)
        + rows(4 * NEAR, 4 * FAR)
        + [
            pltpu.VMEM((4 * R, W), BF16),
            pltpu.VMEM((4 * R, H), F32),
            pltpu.VMEM((4 * R, H), BF16),
            pltpu.VMEM((G, W, H), BF16),
            pltpu.VMEM((G, H, W), BF16),
            pltpu.VMEM((4 * R, W), BF16),
        ]
        + rows(4 * NEAR, 4 * FAR)
        + rows(NEAR, FAR)
        + rows(2 * NEAR, 2 * FAR)
        + rows(NEAR, FAR)
        + rows(NEAR, FAR)
        + [
            pltpu.VMEM((E * B, Q * T), BF16),
            pltpu.VMEM((Q * R, E * B), BF16),
            pltpu.VMEM((E * B, Q * R), BF16),
            pltpu.VMEM((Q * T, E * B), BF16),
            pltpu.VMEM((T, 1), F32),
            pltpu.VMEM((T, D), F32),
            pltpu.VMEM((T, D), BF16),
        ]
        + [dma((G,)), dma((G,)), dma((U,))]
        + [dma((n,)) for n in (U, U, G, G)]
        + [dma((4, n)) for n in (U, U, G, G)]
        + [dma((6, n)) for n in (U, U, G, G)]
        + [dma((n,)) for n in (U, U, G, G)],
        compiler_params=pltpu.CompilerParams(
            collective_id=0, has_side_effects=True, vmem_limit_bytes=62 * 1024 * 1024
        ),
        cost_estimate=pl.CostEstimate(
            flops=16 * R * D * H, bytes_accessed=4 * D * H, transcendentals=T
        ),
    )(tokens, expert_ids.reshape(1, T), slot_ids.reshape(1, T), router.T, w_in, w_out)


def solution(mesh):
    body = fused if mesh.shape["section"] == 4 else per_device
    return jax.shard_map(
        body,
        mesh=mesh,
        in_specs=(
            P(("section", "expert"), None),
            P(("section", "expert")),
            P(("section", "expert")),
            P(),
            P("expert", None, "section"),
            P("expert", "section", None),
        ),
        out_specs=P(("section", "expert"), None),
        check_vma=False,
    )
```

```python
import functools
import math

import jax
import jax.numpy as jnp
from jax import lax
from jax.experimental import pallas as pl
from jax.experimental.pallas import tpu as pltpu
from jax.sharding import PartitionSpec as P

MESH = pl.DeviceIdType.MESH
BF16 = jnp.bfloat16
F32 = jnp.float32
CHUNKS = 8


def per_device(tokens, expert_ids, slot_ids, router, w_in, w_out):
    tok_rows, width_model = tokens.shape
    experts = router.shape[1]
    capacity = 5 * tok_rows // (4 * experts)
    cell_index = expert_ids * capacity + slot_ids
    onehot = (
        cell_index[None, :] == jnp.arange(experts * capacity, dtype=jnp.int32)[:, None]
    ).astype(jnp.bfloat16)
    dispatch = jnp.dot(onehot, tokens, preferred_element_type=jnp.float32).astype(jnp.bfloat16)
    dispatch = dispatch.reshape(experts, capacity, width_model)
    inward = w_in[0]
    outward = w_out[0]
    arrived = lax.all_to_all(dispatch, "expert", split_axis=0, concat_axis=0, tiled=True)
    flat = lax.all_gather(arrived.reshape(-1, width_model), "section", axis=0, tiled=True)
    hidden = jax.nn.relu(jnp.dot(flat, inward, preferred_element_type=jnp.float32)).astype(
        jnp.bfloat16
    )
    summed = lax.psum_scatter(
        jnp.dot(hidden, outward, preferred_element_type=jnp.float32).astype(jnp.bfloat16),
        "section",
        scatter_dimension=0,
        tiled=True,
    )
    expert_out = summed.reshape(experts, capacity, width_model)
    returned = lax.all_to_all(expert_out, "expert", split_axis=0, concat_axis=0, tiled=True)
    combined = lax.dot_general(
        onehot,
        returned.reshape(-1, width_model),
        (((0,), (0,)), ((), ())),
        preferred_element_type=jnp.float32,
    )
    logits = jnp.dot(tokens, router, preferred_element_type=jnp.float32)
    chosen = expert_ids[:, None] == jnp.arange(experts, dtype=jnp.int32)[None, :]
    gating = jax.nn.sigmoid(jnp.sum(jnp.where(chosen, logits, jnp.zeros_like(logits)), axis=1))
    return (gating[:, None] * combined).astype(jnp.bfloat16)


def divide(value, number):
    return lax.shift_right_logical(value * (-(-(1 << 20) // number)), 20)


def iota(shape, dim):
    return lax.broadcasted_iota(jnp.int32, shape, dim)


def one_where(condition):
    return jnp.where(condition, 1.0, 0.0).astype(BF16)


def dot(a, b):
    return jnp.dot(a, b, preferred_element_type=F32)


def kernel(
    dims, tok, eid, sid, router, w_in, w_out, out,
    near_disp, far_disp, near_x, far_x, near_chunk, far_chunk, near_acc, far_acc, near_hid, far_hid, win, wout,
    near_part, far_part, near_half, far_half, near_fin, far_fin,
    near_back, far_back, near_ret, far_ret,
    d_mat, near_p, far_p, near_pt, far_pt, c_mat, gate, comb,
    win_sem, wout_sem,
    near_d_send, near_d_recv, far_d_send, far_d_recv,
    near_g_send, near_g_recv, far_g_send, far_g_recv,
    near_s_send, near_s_recv, far_s_send, far_s_recv,
    near_b_send, near_b_recv, far_b_send, far_b_recv,
):
    E, C, Q, G, U, W, S, T, H, NP, FP = dims
    B, R = Q * C, E * C
    V = G // U
    NEAR, FAR = 2 * V * B, (E - 2) * B
    section, expert = lax.axis_index("section"), lax.axis_index("expert")
    y, x = section // 2, section % 2
    core = expert % 2
    chip = expert - core
    xn = {"section": y * 2 + (1 - x), "expert": expert}
    yn = {"section": (1 - y) * 2 + x, "expert": expert}
    sibling = {"section": section, "expert": chip + 1 - core}
    far = [({"section": section, "expert": (chip + d) % E}, d) for d in range(2, E)]

    def in_copy(c):
        return pltpu.make_async_copy(w_in.at[0, pl.ds(c * W, W)], win.at[c], win_sem.at[c])

    def out_copy(c):
        columns = pl.ds(pl.multiple_of(c * W, W), W)
        return pltpu.make_async_copy(w_out.at[0, :, columns], wout.at[c], wout_sem.at[c])

    def far_start(src, dst, send, recv, c):
        for target, d in far:
            row = pl.multiple_of((core + E - 2 * (d // 2) - 2) * B, 16)
            pltpu.make_async_remote_copy(
                src_ref=src.at[c, pl.ds((d - 2) * B, B)],
                dst_ref=dst.at[c, pl.ds(row, B)],
                send_sem=send.at[c],
                recv_sem=recv.at[c],
                device_id=target,
                device_id_type=MESH,
            ).start()

    def near_start(src, dst, send, recv, u):
        mine = pl.ds(pl.multiple_of(core * (V * B), 16), V * B)
        other = pl.ds(pl.multiple_of((1 - core) * (V * B), 16), V * B)
        pltpu.make_async_remote_copy(
            src_ref=src.at[u, other],
            dst_ref=dst.at[u, mine],
            send_sem=send.at[u],
            recv_sem=recv.at[u],
            device_id=sibling,
            device_id_type=MESH,
        ).start()
        pltpu.make_async_copy(src.at[u, mine], dst.at[u, mine], recv.at[u]).start()

    def await_rows(ref, sem, index, rows):
        view = ref.at[index, pl.ds(0, rows)]
        pltpu.make_async_copy(view, view, sem.at[index]).wait()

    def hop(src, src_row, dst, dst_row, rows, send, recv, index, c, target):
        return pltpu.make_async_remote_copy(
            src_ref=src.at[c, pl.ds(src_row, rows)],
            dst_ref=dst.at[c, pl.ds(dst_row, rows)],
            send_sem=send.at[index, c],
            recv_sem=recv.at[index, c],
            device_id=target,
            device_id_type=MESH,
        )

    def gather_hop(buffers, index, c):
        held, n, send, recv = buffers
        h = n // 2
        src_row, dst_row, rows, target = (
            (0, n, n, xn),
            (0, 2 * n, n, yn),
            (n, 3 * n, h, yn),
            (2 * n + h, 3 * n + h, h, xn),
        )[index]
        return hop(held, src_row, held, dst_row, rows, send, recv, index, c, target)

    def scatter_hop(buffers, index, c):
        part, half, fin, n, send, recv = buffers
        h = n // 2
        src_row, dst, dst_row, target = (
            (3 * n, half, 0, xn),
            (3 * n + h, half, h, yn),
            (n, fin, 0, xn),
            (2 * n + h, fin, n + h, yn),
            (n + h, fin, h, xn),
            (2 * n, fin, n, yn),
        )[index]
        return hop(part, src_row, dst, dst_row, h, send, recv, index, c, target)

    near_g = (near_x, NEAR, near_g_send, near_g_recv)
    far_g = (far_x, FAR, far_g_send, far_g_recv)
    near_s = (near_part, near_half, near_fin, NEAR, near_s_send, near_s_recv)
    far_s = (far_part, far_half, far_fin, FAR, far_s_send, far_s_recv)

    def gather_own(buffers, c):
        gather_hop(buffers, 0, c).start()
        gather_hop(buffers, 1, c).start()

    def gather_relay(buffers, c):
        gather_hop(buffers, 0, c).wait_recv()
        gather_hop(buffers, 2, c).start()
        gather_hop(buffers, 1, c).wait_recv()
        gather_hop(buffers, 3, c).start()

    def gather_rest(buffers, c):
        gather_hop(buffers, 2, c).wait_recv()
        gather_hop(buffers, 3, c).wait_recv()

    def scatter_own(buffers, c):
        for index in range(4):
            scatter_hop(buffers, index, c).start()

    def scatter_relay(buffers, c):
        part, half, _, n, _, _ = buffers
        h = n // 2
        for wait, row, at, send in ((0, 2 * n, 0, 5), (1, n + h, h, 4)):
            scatter_hop(buffers, wait, c).wait_recv()
            part[c, row : row + h] = (
                part[c, row : row + h].astype(F32) + half[c, at : at + h].astype(F32)
            ).astype(BF16)
            scatter_hop(buffers, send, c).start()

    def scatter_total(buffers, c, back):
        part, _, fin, n, _, _ = buffers
        for index in range(2, 6):
            scatter_hop(buffers, index, c).wait_recv()
        back[c] = (
            part[c, 0:n].astype(F32) + fin[c, 0:n].astype(F32) + fin[c, n : 2 * n].astype(F32)
        ).astype(BF16)

    barrier = pltpu.get_barrier_semaphore()
    for target in [target for target, _ in far] + [sibling, xn, yn]:
        pl.semaphore_signal(barrier, inc=1, device_id=target, device_id_type=MESH)

    def keys(shape, dim, first, stride):
        r = iota(shape, dim)
        block = divide(r, B)
        inner = r - block * B
        quarter = divide(inner, C)
        owner = block + first
        owner = jnp.where(owner >= E, owner - E, owner)
        return quarter * stride + owner * C + (inner - quarter * C)

    cell_row = eid[...] * C + sid[...]
    diagonal = iota((T, T), 0) == iota((T, T), 1)

    def column(row):
        spread = jnp.where(diagonal, jnp.broadcast_to(row, (T, T)), 0).astype(F32)
        return jnp.sum(spread, axis=1, keepdims=True).astype(jnp.int32)

    key = keys((E * B, T), 0, chip, R)
    for q in range(Q):
        d_mat[:, q * T : (q + 1) * T] = one_where(key == cell_row + q * R)

    def stacked(c):
        return jnp.concatenate(
            [tok[:, pl.ds(pl.multiple_of(c * W + q * S, S), S)] for q in range(Q)], axis=0
        )

    def far_dispatch(c):
        far_disp[c] = dot(d_mat[2 * B :], stacked(c)).astype(BF16)
        far_start(far_disp, far_x, far_d_send, far_d_recv, c)

    def near_dispatch(u):
        for v in range(V):
            rows = dot(d_mat[0 : 2 * B], stacked(u * V + v)).astype(BF16)
            near_disp[u, v * B : (v + 1) * B] = rows[0:B]
            near_disp[u, (V + v) * B : (V + v + 1) * B] = rows[B : 2 * B]

    near_dispatch(0)
    pl.semaphore_wait(barrier, E + 1)
    near_start(near_disp, near_x, near_d_send, near_d_recv, 0)
    for u in range(1, U):
        near_dispatch(u)
        near_start(near_disp, near_x, near_d_send, near_d_recv, u)
    for u in range(U):
        await_rows(near_x, near_d_recv, u, NEAR)
        gather_own(near_g, u)
        far_dispatch(u)

    @pl.loop(0, G)
    def _(c):
        in_copy(c).start()

    def order(p, pt, rows, stride):
        p[...] = one_where(keys((Q * stride, rows), 1, 0, stride) == iota((Q * stride, rows), 0))
        pt[...] = one_where(keys((rows, Q * stride), 0, 0, stride) == iota((rows, Q * stride), 1))

    order(near_p, near_pt, 2 * B, NP)
    order(far_p, far_pt, FAR, FP)
    near_acc[...] = jnp.zeros_like(near_acc)
    far_acc[...] = jnp.zeros_like(far_acc)

    def widen(raw, p, chunk, stride):
        moved = dot(p[...], jnp.concatenate(raw, axis=1)).astype(BF16)
        for s in range(4):
            for q in range(Q):
                chunk[s * stride : (s + 1) * stride, q * S : (q + 1) * S] = moved[
                    q * stride : (q + 1) * stride, s * S : (s + 1) * S
                ]

    def narrow(chunk, pt, stride):
        rows = [
            jnp.concatenate(
                [chunk[s * stride : (s + 1) * stride, q * S : (q + 1) * S] for s in range(4)],
                axis=1,
            )
            for q in range(Q)
        ]
        return dot(pt[...], jnp.concatenate(rows, axis=0)).astype(BF16)

    def inward(acc, chunk, k):
        @pl.loop(0, H // 256)
        def _(n):
            columns = pl.ds(pl.multiple_of(n * 256, 256), 256)
            acc[:, columns] += dot(chunk[...], win[k, :, columns])

    def activate(acc, hid):
        @pl.loop(0, H // 256)
        def _(n):
            columns = pl.ds(pl.multiple_of(n * 256, 256), 256)
            hid[:, columns] = jnp.maximum(acc[:, columns], 0.0).astype(BF16)

    def outward(hid, chunk, k):
        @pl.loop(0, W // 256)
        def _(n):
            columns = pl.ds(pl.multiple_of(n * 256, 256), 256)
            chunk[:, columns] = dot(hid[...], wout[k, :, columns]).astype(BF16)

    def near_inward(k):
        raw = [jnp.concatenate(near_rows(near_x, k, s * NEAR), axis=0) for s in range(4)]
        widen(raw, near_p, near_chunk, NP)
        in_copy(k).wait()
        inward(near_acc, near_chunk, k)

    def near_outward(k):
        out_copy(k).wait()
        outward(near_hid, near_chunk, k)
        moved = narrow(near_chunk, near_pt, NP)
        u, v = k // V, k % V
        for s in range(4):
            columns = slice(s * S, (s + 1) * S)
            first = pl.multiple_of(s * NEAR + v * B, 16)
            second = pl.multiple_of(s * NEAR + (V + v) * B, 16)
            near_part[u, pl.ds(first, B)] = moved[0:B, columns]
            near_part[u, pl.ds(second, B)] = moved[B : 2 * B, columns]

    def near_rows(ref, k, base):
        u, v = k // V, k % V
        first = pl.multiple_of(base + v * B, 16)
        second = pl.multiple_of(base + (V + v) * B, 16)
        return [ref[u, pl.ds(first, B)], ref[u, pl.ds(second, B)]]

    @pl.loop(0, G + 3)
    def _(c):
        @pl.when(c + 2 < G)
        def _():
            far_dispatch(c + 2)

        @pl.when(c < G)
        def _():
            out_copy(c).start()
            await_rows(far_x, far_d_recv, c, FAR)
            gather_own(far_g, c)

        @pl.when(c < U)
        def _():
            gather_relay(near_g, c)

        @pl.when(c == 0)
        def _():
            key = keys((T, E * B), 1, chip, R)
            cell_column = column(cell_row)
            for q in range(Q):
                c_mat[q * T : (q + 1) * T] = one_where(key == cell_column + q * R)
            logits = lax.dot_general(
                tok[...], router[...], (((1,), (1,)), ((), ())), preferred_element_type=F32
            )
            chosen = column(eid[...]) == iota((T, E), 1)
            picked = jnp.sum(jnp.where(chosen, logits, 0.0), axis=1, keepdims=True)
            gate[...] = 1.0 / (1.0 + jnp.exp(-picked))

        @pl.when((c >= 2) & (c < G + 2))
        def _():
            gather_relay(far_g, c - 2)

        @pl.when(c == 2)
        def _():
            for u in range(U):
                gather_rest(near_g, u)

        @pl.when(c == G + 1)
        def _():
            scatter_own(near_s, 0)

        @pl.when((c >= 3) & (c < 3 + G // 2))
        def _():
            for i in range(2):
                near_inward(2 * (c - 3) + i)

        @pl.when(c == 3 + G // 2)
        def _():
            activate(near_acc, near_hid)

        @pl.when((c >= 3 + G // 2) & (c < 3 + G // 2 + V // 2))
        def _():
            for i in range(2):
                near_outward(2 * (c - 3 - G // 2) + i)

        @pl.when(c >= 3)
        def _():
            k = c - 3
            gather_rest(far_g, k)
            widen([far_x[k, s * FAR : (s + 1) * FAR] for s in range(4)], far_p, far_chunk, FP)
            inward(far_acc, far_chunk, k)

    activate(far_acc, far_hid)

    def combine_near(u):
        await_rows(near_ret, near_b_recv, u, NEAR)
        for v in range(V):
            rows = jnp.concatenate(near_rows(near_ret, u * V + v, 0), axis=0)
            term = dot(c_mat[:, 0 : 2 * B], rows)
            for q in range(Q):
                at = (u * V + v) * W + q * S
                out[:, at : at + S] = (
                    gate[...] * (comb[:, at : at + S] + term[q * T : (q + 1) * T])
                ).astype(BF16)

    def far_own(c):
        outward(far_hid, far_chunk, c)
        moved = narrow(far_chunk, far_pt, FP)
        for s in range(4):
            far_part[c, s * FAR : (s + 1) * FAR] = moved[:, s * S : (s + 1) * S]
        scatter_own(far_s, c)

    def far_total(c):
        scatter_total(far_s, c, far_back)
        far_start(far_back, far_ret, far_b_send, far_b_recv, c)

    def near_total(u):
        scatter_total(near_s, u, near_back)
        near_start(near_back, near_ret, near_b_send, near_b_recv, u)

    def far_combine(c):
        await_rows(far_ret, far_b_recv, c, FAR)
        term = dot(c_mat[:, 2 * B :], far_ret[c])
        for q in range(Q):
            columns = pl.ds(pl.multiple_of(c * W + q * S, S), S)
            comb[:, columns] = term[q * T : (q + 1) * T]

    @pl.loop(0, G + 4)
    def _(c):
        @pl.when(c < G)
        def _():
            far_own(c)

        @pl.when(c == G)
        def _():
            scatter_own(near_s, 1)

        @pl.when(c == 0)
        def _():
            scatter_relay(near_s, 0)

        @pl.when((c >= 2) & (c < G + 2))
        def _():
            scatter_relay(far_s, c - 2)

        @pl.when(c == G + 2)
        def _():
            scatter_relay(near_s, 1)

        @pl.when(c < G - V)
        def _():
            near_outward(V + c)

        @pl.when(c == 2)
        def _():
            near_total(0)

        @pl.when((c >= 3) & (c < G + 3))
        def _():
            far_total(c - 3)

        @pl.when(c == G + 3)
        def _():
            near_total(1)

        @pl.when(c >= 4)
        def _():
            far_combine(c - 4)

        @pl.when(c == G)
        def _():
            combine_near(0)

    combine_near(1)

    @pl.loop(0, G)
    def _(c):
        await_rows(far_disp, far_d_send, c, FAR)
        await_rows(far_back, far_b_send, c, FAR)
        for index in range(4):
            gather_hop(far_g, index, c).wait_send()
        for index in range(6):
            scatter_hop(far_s, index, c).wait_send()

    for u in range(U):
        await_rows(near_disp, near_d_send, u, V * B)
        await_rows(near_back, near_b_send, u, V * B)
        for index in range(4):
            gather_hop(near_g, index, u).wait_send()
        for index in range(6):
            scatter_hop(near_s, index, u).wait_send()


def fused(tokens, expert_ids, slot_ids, router, w_in, w_out):
    T, D = tokens.shape
    E = router.shape[1]
    C = 5 * T // (4 * E)
    H = w_in.shape[2]
    Q = 16 // math.gcd(16, C)
    G = min(CHUNKS, D // (128 * Q))
    U = 2
    W = D // G
    S = W // Q
    B, R = Q * C, E * C
    NEAR, FAR = 2 * (G // U) * B, (E - 2) * B
    NP, FP = -(-2 * C // 16) * 16, -(-(E - 2) * C // 16) * 16
    dims = (E, C, Q, G, U, W, S, T, H, NP, FP)
    vmem = pl.BlockSpec(memory_space=pltpu.VMEM)
    hbm = pl.BlockSpec(memory_space=pl.ANY)
    dma = pltpu.SemaphoreType.DMA
    rows = lambda near, far: [pltpu.VMEM((U, near, S), BF16), pltpu.VMEM((G, far, S), BF16)]
    return pl.pallas_call(
        functools.partial(kernel, dims),
        out_shape=pltpu.VMEM((T, D), BF16),
        in_specs=[vmem, vmem, vmem, vmem, hbm, hbm],
        out_specs=vmem,
        scratch_shapes=rows(NEAR, FAR)
        + rows(4 * NEAR, 4 * FAR)
        + [
            pltpu.VMEM((4 * NP, W), BF16),
            pltpu.VMEM((4 * FP, W), BF16),
            pltpu.VMEM((4 * NP, H), F32),
            pltpu.VMEM((4 * FP, H), F32),
            pltpu.VMEM((4 * NP, H), BF16),
            pltpu.VMEM((4 * FP, H), BF16),
            pltpu.VMEM((G, W, H), BF16),
            pltpu.VMEM((G, H, W), BF16),
        ]
        + rows(4 * NEAR, 4 * FAR)
        + rows(NEAR, FAR)
        + rows(2 * NEAR, 2 * FAR)
        + rows(NEAR, FAR)
        + rows(NEAR, FAR)
        + [
            pltpu.VMEM((E * B, Q * T), BF16),
            pltpu.VMEM((Q * NP, 2 * B), BF16),
            pltpu.VMEM((Q * FP, FAR), BF16),
            pltpu.VMEM((2 * B, Q * NP), BF16),
            pltpu.VMEM((FAR, Q * FP), BF16),
            pltpu.VMEM((Q * T, E * B), BF16),
            pltpu.VMEM((T, 1), F32),
            pltpu.VMEM((T, D), F32),
        ]
        + [dma((G,)), dma((G,))]
        + [dma((n,)) for n in (U, U, G, G)]
        + [dma((4, n)) for n in (U, U, G, G)]
        + [dma((6, n)) for n in (U, U, G, G)]
        + [dma((n,)) for n in (U, U, G, G)],
        compiler_params=pltpu.CompilerParams(
            collective_id=0, has_side_effects=True, vmem_limit_bytes=56 * 1024 * 1024
        ),
        cost_estimate=pl.CostEstimate(
            flops=16 * R * D * H, bytes_accessed=4 * D * H, transcendentals=T
        ),
    )(tokens, expert_ids.reshape(1, T), slot_ids.reshape(1, T), router.T, w_in, w_out)


def solution(mesh):
    body = fused if mesh.shape["section"] == 4 else per_device
    return jax.shard_map(
        body,
        mesh=mesh,
        in_specs=(
            P(("section", "expert"), None),
            P(("section", "expert")),
            P(("section", "expert")),
            P(),
            P("expert", None, "section"),
            P("expert", "section", None),
        ),
        out_specs=P(("section", "expert"), None),
        check_vma=False,
    )
```

```python
import functools
import math

import jax
import jax.numpy as jnp
from jax import lax
from jax.experimental import pallas as pl
from jax.experimental.pallas import tpu as pltpu
from jax.sharding import PartitionSpec as P

MESH = pl.DeviceIdType.MESH
BF16 = jnp.bfloat16
F32 = jnp.float32
CHUNKS = 8


def per_device(tokens, expert_ids, slot_ids, router, w_in, w_out):
    tok_rows, width_model = tokens.shape
    experts = router.shape[1]
    capacity = 5 * tok_rows // (4 * experts)
    cell_index = expert_ids * capacity + slot_ids
    onehot = (
        cell_index[None, :] == jnp.arange(experts * capacity, dtype=jnp.int32)[:, None]
    ).astype(jnp.bfloat16)
    dispatch = jnp.dot(onehot, tokens, preferred_element_type=jnp.float32).astype(jnp.bfloat16)
    dispatch = dispatch.reshape(experts, capacity, width_model)
    inward = w_in[0]
    outward = w_out[0]
    arrived = lax.all_to_all(dispatch, "expert", split_axis=0, concat_axis=0, tiled=True)
    flat = lax.all_gather(arrived.reshape(-1, width_model), "section", axis=0, tiled=True)
    hidden = jax.nn.relu(jnp.dot(flat, inward, preferred_element_type=jnp.float32)).astype(
        jnp.bfloat16
    )
    summed = lax.psum_scatter(
        jnp.dot(hidden, outward, preferred_element_type=jnp.float32).astype(jnp.bfloat16),
        "section",
        scatter_dimension=0,
        tiled=True,
    )
    expert_out = summed.reshape(experts, capacity, width_model)
    returned = lax.all_to_all(expert_out, "expert", split_axis=0, concat_axis=0, tiled=True)
    combined = lax.dot_general(
        onehot,
        returned.reshape(-1, width_model),
        (((0,), (0,)), ((), ())),
        preferred_element_type=jnp.float32,
    )
    logits = jnp.dot(tokens, router, preferred_element_type=jnp.float32)
    chosen = expert_ids[:, None] == jnp.arange(experts, dtype=jnp.int32)[None, :]
    gating = jax.nn.sigmoid(jnp.sum(jnp.where(chosen, logits, jnp.zeros_like(logits)), axis=1))
    return (gating[:, None] * combined).astype(jnp.bfloat16)


def divide(value, number):
    return lax.shift_right_logical(value * (-(-(1 << 20) // number)), 20)


def iota(shape, dim):
    return lax.broadcasted_iota(jnp.int32, shape, dim)


def one_where(condition):
    return jnp.where(condition, 1.0, 0.0).astype(BF16)


def dot(a, b):
    return jnp.dot(a, b, preferred_element_type=F32)


def kernel(
    dims, tok, eid, sid, router, w_in, w_out, out,
    near_disp, far_disp, near_x, far_x, near_chunk, far_chunk, near_acc, far_acc, near_hid, far_hid, win, wout,
    near_part, far_part, near_half, far_half, near_fin, far_fin,
    near_back, far_back, near_ret, far_ret,
    d_mat, near_p, far_p, near_pt, far_pt, c_mat, gate, comb,
    win_sem, wout_sem,
    near_d_send, near_d_recv, far_d_send, far_d_recv,
    near_g_send, near_g_recv, far_g_send, far_g_recv,
    near_s_send, near_s_recv, far_s_send, far_s_recv,
    near_b_send, near_b_recv, far_b_send, far_b_recv,
):
    E, C, Q, G, U, W, S, T, H, NP, FP = dims
    B, R = Q * C, E * C
    V = G // U
    NEAR, FAR = 2 * V * B, (E - 2) * B
    section, expert = lax.axis_index("section"), lax.axis_index("expert")
    y, x = section // 2, section % 2
    core = expert % 2
    chip = expert - core
    xn = {"section": y * 2 + (1 - x), "expert": expert}
    yn = {"section": (1 - y) * 2 + x, "expert": expert}
    sibling = {"section": section, "expert": chip + 1 - core}
    far = [({"section": section, "expert": (chip + d) % E}, d) for d in range(2, E)]

    def in_copy(c):
        return pltpu.make_async_copy(w_in.at[0, pl.ds(c * W, W)], win.at[c], win_sem.at[c])

    def out_copy(c):
        columns = pl.ds(pl.multiple_of(c * W, W), W)
        return pltpu.make_async_copy(w_out.at[0, :, columns], wout.at[c], wout_sem.at[c])

    def far_start(src, dst, send, recv, c):
        for target, d in far:
            row = pl.multiple_of((core + E - 2 * (d // 2) - 2) * B, 16)
            pltpu.make_async_remote_copy(
                src_ref=src.at[c, pl.ds((d - 2) * B, B)],
                dst_ref=dst.at[c, pl.ds(row, B)],
                send_sem=send.at[c],
                recv_sem=recv.at[c],
                device_id=target,
                device_id_type=MESH,
            ).start()

    def near_start(src, dst, send, recv, u):
        mine = pl.ds(pl.multiple_of(core * (V * B), 16), V * B)
        other = pl.ds(pl.multiple_of((1 - core) * (V * B), 16), V * B)
        pltpu.make_async_remote_copy(
            src_ref=src.at[u, other],
            dst_ref=dst.at[u, mine],
            send_sem=send.at[u],
            recv_sem=recv.at[u],
            device_id=sibling,
            device_id_type=MESH,
        ).start()
        pltpu.make_async_copy(src.at[u, mine], dst.at[u, mine], recv.at[u]).start()

    def await_rows(ref, sem, index, rows):
        view = ref.at[index, pl.ds(0, rows)]
        pltpu.make_async_copy(view, view, sem.at[index]).wait()

    def hop(src, src_row, dst, dst_row, rows, send, recv, index, c, target):
        return pltpu.make_async_remote_copy(
            src_ref=src.at[c, pl.ds(src_row, rows)],
            dst_ref=dst.at[c, pl.ds(dst_row, rows)],
            send_sem=send.at[index, c],
            recv_sem=recv.at[index, c],
            device_id=target,
            device_id_type=MESH,
        )

    def gather_hop(buffers, index, c):
        held, n, send, recv = buffers
        h = n // 2
        src_row, dst_row, rows, target = (
            (0, n, n, xn),
            (0, 2 * n, n, yn),
            (n, 3 * n, h, yn),
            (2 * n + h, 3 * n + h, h, xn),
        )[index]
        return hop(held, src_row, held, dst_row, rows, send, recv, index, c, target)

    def scatter_hop(buffers, index, c):
        part, half, fin, n, send, recv = buffers
        h = n // 2
        src_row, dst, dst_row, target = (
            (3 * n, half, 0, xn),
            (3 * n + h, half, h, yn),
            (n, fin, 0, xn),
            (2 * n + h, fin, n + h, yn),
            (n + h, fin, h, xn),
            (2 * n, fin, n, yn),
        )[index]
        return hop(part, src_row, dst, dst_row, h, send, recv, index, c, target)

    near_g = (near_x, NEAR, near_g_send, near_g_recv)
    far_g = (far_x, FAR, far_g_send, far_g_recv)
    near_s = (near_part, near_half, near_fin, NEAR, near_s_send, near_s_recv)
    far_s = (far_part, far_half, far_fin, FAR, far_s_send, far_s_recv)

    def gather_own(buffers, c):
        gather_hop(buffers, 0, c).start()
        gather_hop(buffers, 1, c).start()

    def gather_relay(buffers, c):
        gather_hop(buffers, 0, c).wait_recv()
        gather_hop(buffers, 2, c).start()
        gather_hop(buffers, 1, c).wait_recv()
        gather_hop(buffers, 3, c).start()

    def gather_rest(buffers, c):
        gather_hop(buffers, 2, c).wait_recv()
        gather_hop(buffers, 3, c).wait_recv()

    def scatter_own(buffers, c):
        for index in range(4):
            scatter_hop(buffers, index, c).start()

    def scatter_relay(buffers, c):
        part, half, _, n, _, _ = buffers
        h = n // 2
        for wait, row, at, send in ((0, 2 * n, 0, 5), (1, n + h, h, 4)):
            scatter_hop(buffers, wait, c).wait_recv()
            part[c, row : row + h] = (
                part[c, row : row + h].astype(F32) + half[c, at : at + h].astype(F32)
            ).astype(BF16)
            scatter_hop(buffers, send, c).start()

    def scatter_total(buffers, c, back):
        part, _, fin, n, _, _ = buffers
        for index in range(2, 6):
            scatter_hop(buffers, index, c).wait_recv()
        back[c] = (
            part[c, 0:n].astype(F32) + fin[c, 0:n].astype(F32) + fin[c, n : 2 * n].astype(F32)
        ).astype(BF16)

    barrier = pltpu.get_barrier_semaphore()
    for target in [target for target, _ in far] + [sibling, xn, yn]:
        pl.semaphore_signal(barrier, inc=1, device_id=target, device_id_type=MESH)

    def keys(shape, dim, first, stride):
        r = iota(shape, dim)
        block = divide(r, B)
        inner = r - block * B
        quarter = divide(inner, C)
        owner = block + first
        owner = jnp.where(owner >= E, owner - E, owner)
        return quarter * stride + owner * C + (inner - quarter * C)

    cell_row = eid[...] * C + sid[...]
    diagonal = iota((T, T), 0) == iota((T, T), 1)

    def column(row):
        spread = jnp.where(diagonal, jnp.broadcast_to(row, (T, T)), 0).astype(F32)
        return jnp.sum(spread, axis=1, keepdims=True).astype(jnp.int32)

    key = keys((E * B, T), 0, chip, R)
    for q in range(Q):
        d_mat[:, q * T : (q + 1) * T] = one_where(key == cell_row + q * R)

    def stacked(c):
        return jnp.concatenate(
            [tok[:, pl.ds(pl.multiple_of(c * W + q * S, S), S)] for q in range(Q)], axis=0
        )

    def far_dispatch(c):
        far_disp[c] = dot(d_mat[2 * B :], stacked(c)).astype(BF16)
        far_start(far_disp, far_x, far_d_send, far_d_recv, c)

    def near_dispatch(u):
        for v in range(V):
            rows = dot(d_mat[0 : 2 * B], stacked(u * V + v)).astype(BF16)
            near_disp[u, v * B : (v + 1) * B] = rows[0:B]
            near_disp[u, (V + v) * B : (V + v + 1) * B] = rows[B : 2 * B]

    near_dispatch(0)
    pl.semaphore_wait(barrier, E + 1)
    near_start(near_disp, near_x, near_d_send, near_d_recv, 0)
    for u in range(1, U):
        near_dispatch(u)
        near_start(near_disp, near_x, near_d_send, near_d_recv, u)
    for u in range(U):
        await_rows(near_x, near_d_recv, u, NEAR)
        gather_own(near_g, u)
        far_dispatch(u)

    @pl.loop(0, G)
    def _(c):
        in_copy(c).start()

    def order(p, pt, rows, stride):
        p[...] = one_where(keys((Q * stride, rows), 1, 0, stride) == iota((Q * stride, rows), 0))
        pt[...] = one_where(keys((rows, Q * stride), 0, 0, stride) == iota((rows, Q * stride), 1))

    order(near_p, near_pt, 2 * B, NP)
    order(far_p, far_pt, FAR, FP)
    near_acc[...] = jnp.zeros_like(near_acc)
    far_acc[...] = jnp.zeros_like(far_acc)

    def widen(raw, p, chunk, stride):
        moved = dot(p[...], jnp.concatenate(raw, axis=1)).astype(BF16)
        for s in range(4):
            for q in range(Q):
                chunk[s * stride : (s + 1) * stride, q * S : (q + 1) * S] = moved[
                    q * stride : (q + 1) * stride, s * S : (s + 1) * S
                ]

    def narrow(chunk, pt, stride):
        rows = [
            jnp.concatenate(
                [chunk[s * stride : (s + 1) * stride, q * S : (q + 1) * S] for s in range(4)],
                axis=1,
            )
            for q in range(Q)
        ]
        return dot(pt[...], jnp.concatenate(rows, axis=0)).astype(BF16)

    def inward(acc, chunk, k):
        @pl.loop(0, H // 256)
        def _(n):
            columns = pl.ds(pl.multiple_of(n * 256, 256), 256)
            acc[:, columns] += dot(chunk[...], win[k, :, columns])

    def activate(acc, hid):
        @pl.loop(0, H // 256)
        def _(n):
            columns = pl.ds(pl.multiple_of(n * 256, 256), 256)
            hid[:, columns] = jnp.maximum(acc[:, columns], 0.0).astype(BF16)

    def outward(hid, chunk, k):
        @pl.loop(0, W // 256)
        def _(n):
            columns = pl.ds(pl.multiple_of(n * 256, 256), 256)
            chunk[:, columns] = dot(hid[...], wout[k, :, columns]).astype(BF16)

    def near_inward(k):
        raw = [jnp.concatenate(near_rows(near_x, k, s * NEAR), axis=0) for s in range(4)]
        widen(raw, near_p, near_chunk, NP)
        in_copy(k).wait()
        inward(near_acc, near_chunk, k)

    def near_outward(k):
        out_copy(k).wait()
        outward(near_hid, near_chunk, k)
        moved = narrow(near_chunk, near_pt, NP)
        u, v = k // V, k % V
        for s in range(4):
            columns = slice(s * S, (s + 1) * S)
            first = pl.multiple_of(s * NEAR + v * B, 16)
            second = pl.multiple_of(s * NEAR + (V + v) * B, 16)
            near_part[u, pl.ds(first, B)] = moved[0:B, columns]
            near_part[u, pl.ds(second, B)] = moved[B : 2 * B, columns]

    def near_rows(ref, k, base):
        u, v = k // V, k % V
        first = pl.multiple_of(base + v * B, 16)
        second = pl.multiple_of(base + (V + v) * B, 16)
        return [ref[u, pl.ds(first, B)], ref[u, pl.ds(second, B)]]

    @pl.loop(0, G + 4)
    def _(c):
        @pl.when(c + 2 < G)
        def _():
            far_dispatch(c + 2)

        @pl.when(c < G)
        def _():
            out_copy(c).start()
            await_rows(far_x, far_d_recv, c, FAR)
            gather_own(far_g, c)

        @pl.when(c < U)
        def _():
            gather_relay(near_g, c)

        @pl.when(c == 0)
        def _():
            key = keys((T, E * B), 1, chip, R)
            cell_column = column(cell_row)
            for q in range(Q):
                c_mat[q * T : (q + 1) * T] = one_where(key == cell_column + q * R)
            logits = lax.dot_general(
                tok[...], router[...], (((1,), (1,)), ((), ())), preferred_element_type=F32
            )
            chosen = column(eid[...]) == iota((T, E), 1)
            picked = jnp.sum(jnp.where(chosen, logits, 0.0), axis=1, keepdims=True)
            gate[...] = 1.0 / (1.0 + jnp.exp(-picked))

        @pl.when((c >= 2) & (c < G + 2))
        def _():
            gather_relay(far_g, c - 2)

        @pl.when(c == 3)
        def _():
            for u in range(U):
                gather_rest(near_g, u)

        @pl.when(c == G + 2)
        def _():
            scatter_own(near_s, 0)

        @pl.when((c >= 4) & (c < 4 + G // 2))
        def _():
            for i in range(2):
                near_inward(2 * (c - 4) + i)

        @pl.when(c == 4 + G // 2)
        def _():
            activate(near_acc, near_hid)

        @pl.when((c >= 4 + G // 2) & (c < 4 + G // 2 + V // 2))
        def _():
            for i in range(2):
                near_outward(2 * (c - 4 - G // 2) + i)

        @pl.when(c >= 4)
        def _():
            k = c - 4
            gather_rest(far_g, k)
            widen([far_x[k, s * FAR : (s + 1) * FAR] for s in range(4)], far_p, far_chunk, FP)
            inward(far_acc, far_chunk, k)

    activate(far_acc, far_hid)

    def combine_near(u):
        await_rows(near_ret, near_b_recv, u, NEAR)
        for v in range(V):
            rows = jnp.concatenate(near_rows(near_ret, u * V + v, 0), axis=0)
            term = dot(c_mat[:, 0 : 2 * B], rows)
            for q in range(Q):
                at = (u * V + v) * W + q * S
                out[:, at : at + S] = (
                    gate[...] * (comb[:, at : at + S] + term[q * T : (q + 1) * T])
                ).astype(BF16)

    def far_own(c):
        outward(far_hid, far_chunk, c)
        moved = narrow(far_chunk, far_pt, FP)
        for s in range(4):
            far_part[c, s * FAR : (s + 1) * FAR] = moved[:, s * S : (s + 1) * S]
        scatter_own(far_s, c)

    def far_total(c):
        scatter_total(far_s, c, far_back)
        far_start(far_back, far_ret, far_b_send, far_b_recv, c)

    def near_total(u):
        scatter_total(near_s, u, near_back)
        near_start(near_back, near_ret, near_b_send, near_b_recv, u)

    def far_combine(c):
        await_rows(far_ret, far_b_recv, c, FAR)
        term = dot(c_mat[:, 2 * B :], far_ret[c])
        for q in range(Q):
            columns = pl.ds(pl.multiple_of(c * W + q * S, S), S)
            comb[:, columns] = term[q * T : (q + 1) * T]

    @pl.loop(0, G + 5)
    def _(c):
        @pl.when(c < G)
        def _():
            far_own(c)

        @pl.when(c == G)
        def _():
            scatter_own(near_s, 1)

        @pl.when(c == 0)
        def _():
            scatter_relay(near_s, 0)

        @pl.when((c >= 2) & (c < G + 2))
        def _():
            scatter_relay(far_s, c - 2)

        @pl.when(c == G + 2)
        def _():
            scatter_relay(near_s, 1)

        @pl.when(c < G - V)
        def _():
            near_outward(V + c)

        @pl.when(c == 3)
        def _():
            near_total(0)

        @pl.when((c >= 4) & (c < G + 4))
        def _():
            far_total(c - 4)

        @pl.when(c == G + 4)
        def _():
            near_total(1)

        @pl.when(c >= 5)
        def _():
            far_combine(c - 5)

        @pl.when(c == G)
        def _():
            combine_near(0)

    combine_near(1)

    @pl.loop(0, G)
    def _(c):
        await_rows(far_disp, far_d_send, c, FAR)
        await_rows(far_back, far_b_send, c, FAR)
        for index in range(4):
            gather_hop(far_g, index, c).wait_send()
        for index in range(6):
            scatter_hop(far_s, index, c).wait_send()

    for u in range(U):
        await_rows(near_disp, near_d_send, u, V * B)
        await_rows(near_back, near_b_send, u, V * B)
        for index in range(4):
            gather_hop(near_g, index, u).wait_send()
        for index in range(6):
            scatter_hop(near_s, index, u).wait_send()


def fused(tokens, expert_ids, slot_ids, router, w_in, w_out):
    T, D = tokens.shape
    E = router.shape[1]
    C = 5 * T // (4 * E)
    H = w_in.shape[2]
    Q = 16 // math.gcd(16, C)
    G = min(CHUNKS, D // (128 * Q))
    U = 2
    W = D // G
    S = W // Q
    B, R = Q * C, E * C
    NEAR, FAR = 2 * (G // U) * B, (E - 2) * B
    NP, FP = -(-2 * C // 16) * 16, -(-(E - 2) * C // 16) * 16
    dims = (E, C, Q, G, U, W, S, T, H, NP, FP)
    vmem = pl.BlockSpec(memory_space=pltpu.VMEM)
    hbm = pl.BlockSpec(memory_space=pl.ANY)
    dma = pltpu.SemaphoreType.DMA
    rows = lambda near, far: [pltpu.VMEM((U, near, S), BF16), pltpu.VMEM((G, far, S), BF16)]
    return pl.pallas_call(
        functools.partial(kernel, dims),
        out_shape=pltpu.VMEM((T, D), BF16),
        in_specs=[vmem, vmem, vmem, vmem, hbm, hbm],
        out_specs=vmem,
        scratch_shapes=rows(NEAR, FAR)
        + rows(4 * NEAR, 4 * FAR)
        + [
            pltpu.VMEM((4 * NP, W), BF16),
            pltpu.VMEM((4 * FP, W), BF16),
            pltpu.VMEM((4 * NP, H), F32),
            pltpu.VMEM((4 * FP, H), F32),
            pltpu.VMEM((4 * NP, H), BF16),
            pltpu.VMEM((4 * FP, H), BF16),
            pltpu.VMEM((G, W, H), BF16),
            pltpu.VMEM((G, H, W), BF16),
        ]
        + rows(4 * NEAR, 4 * FAR)
        + rows(NEAR, FAR)
        + rows(2 * NEAR, 2 * FAR)
        + rows(NEAR, FAR)
        + rows(NEAR, FAR)
        + [
            pltpu.VMEM((E * B, Q * T), BF16),
            pltpu.VMEM((Q * NP, 2 * B), BF16),
            pltpu.VMEM((Q * FP, FAR), BF16),
            pltpu.VMEM((2 * B, Q * NP), BF16),
            pltpu.VMEM((FAR, Q * FP), BF16),
            pltpu.VMEM((Q * T, E * B), BF16),
            pltpu.VMEM((T, 1), F32),
            pltpu.VMEM((T, D), F32),
        ]
        + [dma((G,)), dma((G,))]
        + [dma((n,)) for n in (U, U, G, G)]
        + [dma((4, n)) for n in (U, U, G, G)]
        + [dma((6, n)) for n in (U, U, G, G)]
        + [dma((n,)) for n in (U, U, G, G)],
        compiler_params=pltpu.CompilerParams(
            collective_id=0, has_side_effects=True, vmem_limit_bytes=56 * 1024 * 1024
        ),
        cost_estimate=pl.CostEstimate(
            flops=16 * R * D * H, bytes_accessed=4 * D * H, transcendentals=T
        ),
    )(tokens, expert_ids.reshape(1, T), slot_ids.reshape(1, T), router.T, w_in, w_out)


def solution(mesh):
    body = fused if mesh.shape["section"] == 4 else per_device
    return jax.shard_map(
        body,
        mesh=mesh,
        in_specs=(
            P(("section", "expert"), None),
            P(("section", "expert")),
            P(("section", "expert")),
            P(),
            P("expert", None, "section"),
            P("expert", "section", None),
        ),
        out_specs=P(("section", "expert"), None),
        check_vma=False,
    )
```

```python
import functools
import math

import jax
import jax.numpy as jnp
from jax import lax
from jax.experimental import pallas as pl
from jax.experimental.pallas import tpu as pltpu
from jax.sharding import PartitionSpec as P

MESH = pl.DeviceIdType.MESH
BF16 = jnp.bfloat16
F32 = jnp.float32
CHUNKS = 8


def per_device(tokens, expert_ids, slot_ids, router, w_in, w_out):
    tok_rows, width_model = tokens.shape
    experts = router.shape[1]
    capacity = 5 * tok_rows // (4 * experts)
    cell_index = expert_ids * capacity + slot_ids
    onehot = (
        cell_index[None, :] == jnp.arange(experts * capacity, dtype=jnp.int32)[:, None]
    ).astype(jnp.bfloat16)
    dispatch = jnp.dot(onehot, tokens, preferred_element_type=jnp.float32).astype(jnp.bfloat16)
    dispatch = dispatch.reshape(experts, capacity, width_model)
    inward = w_in[0]
    outward = w_out[0]
    arrived = lax.all_to_all(dispatch, "expert", split_axis=0, concat_axis=0, tiled=True)
    flat = lax.all_gather(arrived.reshape(-1, width_model), "section", axis=0, tiled=True)
    hidden = jax.nn.relu(jnp.dot(flat, inward, preferred_element_type=jnp.float32)).astype(
        jnp.bfloat16
    )
    summed = lax.psum_scatter(
        jnp.dot(hidden, outward, preferred_element_type=jnp.float32).astype(jnp.bfloat16),
        "section",
        scatter_dimension=0,
        tiled=True,
    )
    expert_out = summed.reshape(experts, capacity, width_model)
    returned = lax.all_to_all(expert_out, "expert", split_axis=0, concat_axis=0, tiled=True)
    combined = lax.dot_general(
        onehot,
        returned.reshape(-1, width_model),
        (((0,), (0,)), ((), ())),
        preferred_element_type=jnp.float32,
    )
    logits = jnp.dot(tokens, router, preferred_element_type=jnp.float32)
    chosen = expert_ids[:, None] == jnp.arange(experts, dtype=jnp.int32)[None, :]
    gating = jax.nn.sigmoid(jnp.sum(jnp.where(chosen, logits, jnp.zeros_like(logits)), axis=1))
    return (gating[:, None] * combined).astype(jnp.bfloat16)


def divide(value, number):
    return lax.shift_right_logical(value * (-(-(1 << 20) // number)), 20)


def iota(shape, dim):
    return lax.broadcasted_iota(jnp.int32, shape, dim)


def one_where(condition):
    return jnp.where(condition, 1.0, 0.0).astype(BF16)


def dot(a, b):
    return jnp.dot(a, b, preferred_element_type=F32)


def kernel(
    dims, tok_hbm, eid_hbm, sid_hbm, router_hbm, w_in, w_out, out,
    tok, eid, sid, router,
    near_disp, far_disp, near_x, far_x, near_chunk, far_chunk, near_acc, far_acc, near_hid, far_hid, win, wout,
    near_part, far_part, near_half, far_half, near_fin, far_fin,
    near_back, far_back, near_ret, far_ret,
    d_mat, near_p, far_p, near_pt, far_pt, c_mat, gate, comb,
    win_sem, wout_sem, load_sem, tok_sem,
    near_d_send, near_d_recv, far_d_send, far_d_recv,
    near_g_send, near_g_recv, far_g_send, far_g_recv,
    near_s_send, near_s_recv, far_s_send, far_s_recv,
    near_b_send, near_b_recv, far_b_send, far_b_recv,
):
    E, C, Q, G, U, W, S, T, H, NP, FP = dims
    B, R = Q * C, E * C
    V = G // U
    NEAR, FAR = 2 * V * B, (E - 2) * B
    section, expert = lax.axis_index("section"), lax.axis_index("expert")
    y, x = section // 2, section % 2
    core = expert % 2
    chip = expert - core
    xn = {"section": y * 2 + (1 - x), "expert": expert}
    yn = {"section": (1 - y) * 2 + x, "expert": expert}
    sibling = {"section": section, "expert": chip + 1 - core}
    far = [({"section": section, "expert": (chip + d) % E}, d) for d in range(2, E)]

    def in_copy(c):
        return pltpu.make_async_copy(w_in.at[0, pl.ds(c * W, W)], win.at[c], win_sem.at[c])

    def out_copy(c):
        columns = pl.ds(pl.multiple_of(c * W, W), W)
        return pltpu.make_async_copy(w_out.at[0, :, columns], wout.at[c], wout_sem.at[c])

    def far_start(src, dst, send, recv, c):
        for target, d in far:
            row = pl.multiple_of((core + E - 2 * (d // 2) - 2) * B, 16)
            pltpu.make_async_remote_copy(
                src_ref=src.at[c, pl.ds((d - 2) * B, B)],
                dst_ref=dst.at[c, pl.ds(row, B)],
                send_sem=send.at[c],
                recv_sem=recv.at[c],
                device_id=target,
                device_id_type=MESH,
            ).start()

    def near_start(src, dst, send, recv, u):
        mine = pl.ds(pl.multiple_of(core * (V * B), 16), V * B)
        other = pl.ds(pl.multiple_of((1 - core) * (V * B), 16), V * B)
        pltpu.make_async_remote_copy(
            src_ref=src.at[u, other],
            dst_ref=dst.at[u, mine],
            send_sem=send.at[u],
            recv_sem=recv.at[u],
            device_id=sibling,
            device_id_type=MESH,
        ).start()
        pltpu.make_async_copy(src.at[u, mine], dst.at[u, mine], recv.at[u]).start()

    def await_rows(ref, sem, index, rows):
        view = ref.at[index, pl.ds(0, rows)]
        pltpu.make_async_copy(view, view, sem.at[index]).wait()

    def hop(src, src_row, dst, dst_row, rows, send, recv, index, c, target):
        return pltpu.make_async_remote_copy(
            src_ref=src.at[c, pl.ds(src_row, rows)],
            dst_ref=dst.at[c, pl.ds(dst_row, rows)],
            send_sem=send.at[index, c],
            recv_sem=recv.at[index, c],
            device_id=target,
            device_id_type=MESH,
        )

    def gather_hop(buffers, index, c):
        held, n, send, recv = buffers
        h = n // 2
        src_row, dst_row, rows, target = (
            (0, n, n, xn),
            (0, 2 * n, n, yn),
            (n, 3 * n, h, yn),
            (2 * n + h, 3 * n + h, h, xn),
        )[index]
        return hop(held, src_row, held, dst_row, rows, send, recv, index, c, target)

    def near_hop(index, u):
        own = pl.multiple_of(core * (V * B), 16)
        other = pl.multiple_of((1 - core) * (V * B), 16)
        src, src_row, target, base = (
            (near_disp, own, xn, NEAR),
            (near_disp, own, yn, 2 * NEAR),
            (near_x, other, xn, NEAR),
            (near_x, other, yn, 2 * NEAR),
            (near_x, NEAR, yn, 3 * NEAR),
            (near_x, 2 * NEAR + V * B, xn, 3 * NEAR + V * B),
        )[index]
        dst_row = base if index >= 4 else base + src_row
        if index < 4:
            dst_row = pl.multiple_of(dst_row, 16)
        return hop(
            src, src_row, near_x, dst_row, V * B, near_g_send, near_g_recv, index, u, target
        )

    def scatter_hop(buffers, index, c):
        part, half, fin, n, send, recv = buffers
        h = n // 2
        src_row, dst, dst_row, target = (
            (3 * n, half, 0, xn),
            (3 * n + h, half, h, yn),
            (n, fin, 0, xn),
            (2 * n + h, fin, n + h, yn),
            (n + h, fin, h, xn),
            (2 * n, fin, n, yn),
        )[index]
        return hop(part, src_row, dst, dst_row, h, send, recv, index, c, target)

    far_g = (far_x, FAR, far_g_send, far_g_recv)
    near_s = (near_part, near_half, near_fin, NEAR, near_s_send, near_s_recv)
    far_s = (far_part, far_half, far_fin, FAR, far_s_send, far_s_recv)

    def gather_own(buffers, c):
        gather_hop(buffers, 0, c).start()
        gather_hop(buffers, 1, c).start()

    def gather_relay(buffers, c):
        gather_hop(buffers, 0, c).wait_recv()
        gather_hop(buffers, 2, c).start()
        gather_hop(buffers, 1, c).wait_recv()
        gather_hop(buffers, 3, c).start()

    def gather_rest(buffers, c):
        gather_hop(buffers, 2, c).wait_recv()
        gather_hop(buffers, 3, c).wait_recv()

    def scatter_own(buffers, c):
        for index in range(4):
            scatter_hop(buffers, index, c).start()

    def scatter_relay(buffers, c):
        part, half, _, n, _, _ = buffers
        h = n // 2
        for wait, row, at, send in ((0, 2 * n, 0, 5), (1, n + h, h, 4)):
            scatter_hop(buffers, wait, c).wait_recv()
            part[c, row : row + h] = (
                part[c, row : row + h].astype(F32) + half[c, at : at + h].astype(F32)
            ).astype(BF16)
            scatter_hop(buffers, send, c).start()

    def scatter_total(buffers, c, back):
        part, _, fin, n, _, _ = buffers
        for index in range(2, 6):
            scatter_hop(buffers, index, c).wait_recv()
        back[c] = (
            part[c, 0:n].astype(F32) + fin[c, 0:n].astype(F32) + fin[c, n : 2 * n].astype(F32)
        ).astype(BF16)

    barrier = pltpu.get_barrier_semaphore()
    for target in [target for target, _ in far] + [sibling, xn, yn]:
        pl.semaphore_signal(barrier, inc=1, device_id=target, device_id_type=MESH)

    loads = [
        pltpu.make_async_copy(src, dst, load_sem.at[i])
        for i, (src, dst) in enumerate(((eid_hbm, eid), (sid_hbm, sid), (router_hbm, router)))
    ]
    halves = [slice(u * V * W, (u + 1) * V * W) for u in range(U)]
    tok_loads = [
        pltpu.make_async_copy(tok_hbm.at[:, part], tok.at[:, part], tok_sem.at[u])
        for u, part in enumerate(halves)
    ]
    for copy in loads[0:2] + tok_loads + loads[2:]:
        copy.start()
    loads[0].wait()
    loads[1].wait()

    def keys(shape, dim, first, stride):
        r = iota(shape, dim)
        block = divide(r, B)
        inner = r - block * B
        quarter = divide(inner, C)
        owner = block + first
        owner = jnp.where(owner >= E, owner - E, owner)
        return quarter * stride + owner * C + (inner - quarter * C)

    cell_row = eid[...] * C + sid[...]
    diagonal = iota((T, T), 0) == iota((T, T), 1)

    def column(row):
        spread = jnp.where(diagonal, jnp.broadcast_to(row, (T, T)), 0).astype(F32)
        return jnp.sum(spread, axis=1, keepdims=True).astype(jnp.int32)

    key = keys((E * B, T), 0, chip, R)
    for q in range(Q):
        d_mat[:, q * T : (q + 1) * T] = one_where(key == cell_row + q * R)

    def stacked(c):
        return jnp.concatenate(
            [tok[:, pl.ds(pl.multiple_of(c * W + q * S, S), S)] for q in range(Q)], axis=0
        )

    def far_dispatch(c):
        far_disp[c] = dot(d_mat[2 * B :], stacked(c)).astype(BF16)
        far_start(far_disp, far_x, far_d_send, far_d_recv, c)

    def near_dispatch(u):
        tok_loads[u].wait()
        for v in range(V):
            rows = dot(d_mat[0 : 2 * B], stacked(u * V + v)).astype(BF16)
            near_disp[u, v * B : (v + 1) * B] = rows[0:B]
            near_disp[u, (V + v) * B : (V + v + 1) * B] = rows[B : 2 * B]

    def near_begin(u):
        near_start(near_disp, near_x, near_d_send, near_d_recv, u)
        near_hop(0, u).start()
        near_hop(1, u).start()

    near_dispatch(0)
    pl.semaphore_wait(barrier, E + 1)
    near_begin(0)
    for u in range(1, U):
        near_dispatch(u)
        near_begin(u)
    for u in range(U):
        await_rows(near_x, near_d_recv, u, NEAR)
        near_hop(2, u).start()
        near_hop(3, u).start()
        far_dispatch(u)

    @pl.loop(0, G)
    def _(c):
        in_copy(c).start()

    def order(p, pt, rows, stride):
        p[...] = one_where(keys((Q * stride, rows), 1, 0, stride) == iota((Q * stride, rows), 0))
        pt[...] = one_where(keys((rows, Q * stride), 0, 0, stride) == iota((rows, Q * stride), 1))

    order(near_p, near_pt, 2 * B, NP)
    order(far_p, far_pt, FAR, FP)
    near_acc[...] = jnp.zeros_like(near_acc)
    far_acc[...] = jnp.zeros_like(far_acc)

    def widen(raw, p, chunk, stride):
        moved = dot(p[...], jnp.concatenate(raw, axis=1)).astype(BF16)
        for s in range(4):
            for q in range(Q):
                chunk[s * stride : (s + 1) * stride, q * S : (q + 1) * S] = moved[
                    q * stride : (q + 1) * stride, s * S : (s + 1) * S
                ]

    def narrow(chunk, pt, stride):
        rows = [
            jnp.concatenate(
                [chunk[s * stride : (s + 1) * stride, q * S : (q + 1) * S] for s in range(4)],
                axis=1,
            )
            for q in range(Q)
        ]
        return dot(pt[...], jnp.concatenate(rows, axis=0)).astype(BF16)

    def inward(acc, chunk, k):
        @pl.loop(0, H // 256)
        def _(n):
            columns = pl.ds(pl.multiple_of(n * 256, 256), 256)
            acc[:, columns] += dot(chunk[...], win[k, :, columns])

    def activate(acc, hid):
        @pl.loop(0, H // 256)
        def _(n):
            columns = pl.ds(pl.multiple_of(n * 256, 256), 256)
            hid[:, columns] = jnp.maximum(acc[:, columns], 0.0).astype(BF16)

    def outward(hid, chunk, k):
        @pl.loop(0, W // 256)
        def _(n):
            columns = pl.ds(pl.multiple_of(n * 256, 256), 256)
            chunk[:, columns] = dot(hid[...], wout[k, :, columns]).astype(BF16)

    def near_inward(k):
        raw = [jnp.concatenate(near_rows(near_x, k, s * NEAR), axis=0) for s in range(4)]
        widen(raw, near_p, near_chunk, NP)
        in_copy(k).wait()
        inward(near_acc, near_chunk, k)

    def near_outward(k):
        out_copy(k).wait()
        outward(near_hid, near_chunk, k)
        moved = narrow(near_chunk, near_pt, NP)
        u, v = k // V, k % V
        for s in range(4):
            columns = slice(s * S, (s + 1) * S)
            first = pl.multiple_of(s * NEAR + v * B, 16)
            second = pl.multiple_of(s * NEAR + (V + v) * B, 16)
            near_part[u, pl.ds(first, B)] = moved[0:B, columns]
            near_part[u, pl.ds(second, B)] = moved[B : 2 * B, columns]

    def near_rows(ref, k, base):
        u, v = k // V, k % V
        first = pl.multiple_of(base + v * B, 16)
        second = pl.multiple_of(base + (V + v) * B, 16)
        return [ref[u, pl.ds(first, B)], ref[u, pl.ds(second, B)]]

    @pl.loop(0, G + 4)
    def _(c):
        @pl.when(c + 2 < G)
        def _():
            far_dispatch(c + 2)

        @pl.when(c < G)
        def _():
            out_copy(c).start()
            await_rows(far_x, far_d_recv, c, FAR)
            gather_own(far_g, c)

        @pl.when(c < U)
        def _():
            near_hop(0, c).wait_recv()
            near_hop(2, c).wait_recv()
            near_hop(4, c).start()
            near_hop(1, c).wait_recv()
            near_hop(3, c).wait_recv()
            near_hop(5, c).start()

        @pl.when(c == 0)
        def _():
            key = keys((T, E * B), 1, chip, R)
            cell_column = column(cell_row)
            for q in range(Q):
                c_mat[q * T : (q + 1) * T] = one_where(key == cell_column + q * R)
            loads[2].wait()
            logits = lax.dot_general(
                tok[...], router[...], (((1,), (1,)), ((), ())), preferred_element_type=F32
            )
            chosen = column(eid[...]) == iota((T, E), 1)
            picked = jnp.sum(jnp.where(chosen, logits, 0.0), axis=1, keepdims=True)
            gate[...] = 1.0 / (1.0 + jnp.exp(-picked))

        @pl.when((c >= 2) & (c < G + 2))
        def _():
            gather_relay(far_g, c - 2)

        @pl.when(c == 3)
        def _():
            for u in range(U):
                near_hop(4, u).wait_recv()
                near_hop(5, u).wait_recv()

        @pl.when((c >= 4) & (c < 4 + G // 2))
        def _():
            for i in range(2):
                near_inward(2 * (c - 4) + i)

        @pl.when(c == 4 + G // 2)
        def _():
            activate(near_acc, near_hid)

        @pl.when((c >= 4 + G // 2) & (c < 4 + G // 2 + V // 2))
        def _():
            for i in range(2):
                near_outward(2 * (c - 4 - G // 2) + i)

        @pl.when(c == 3 + G // 2 + V // 2)
        def _():
            scatter_own(near_s, 0)

        @pl.when(c >= 4)
        def _():
            k = c - 4
            gather_rest(far_g, k)
            widen([far_x[k, s * FAR : (s + 1) * FAR] for s in range(4)], far_p, far_chunk, FP)
            inward(far_acc, far_chunk, k)

    activate(far_acc, far_hid)

    def combine_near(u):
        await_rows(near_ret, near_b_recv, u, NEAR)
        for v in range(V):
            rows = jnp.concatenate(near_rows(near_ret, u * V + v, 0), axis=0)
            term = dot(c_mat[:, 0 : 2 * B], rows)
            for q in range(Q):
                at = (u * V + v) * W + q * S
                out[:, at : at + S] = (
                    gate[...] * (comb[:, at : at + S] + term[q * T : (q + 1) * T])
                ).astype(BF16)

    def far_own(c):
        outward(far_hid, far_chunk, c)
        moved = narrow(far_chunk, far_pt, FP)
        for s in range(4):
            far_part[c, s * FAR : (s + 1) * FAR] = moved[:, s * S : (s + 1) * S]
        scatter_own(far_s, c)

    def far_total(c):
        scatter_total(far_s, c, far_back)
        far_start(far_back, far_ret, far_b_send, far_b_recv, c)

    def near_total(u):
        scatter_total(near_s, u, near_back)
        near_start(near_back, near_ret, near_b_send, near_b_recv, u)

    def far_combine(c):
        await_rows(far_ret, far_b_recv, c, FAR)
        term = dot(c_mat[:, 2 * B :], far_ret[c])
        for q in range(Q):
            columns = pl.ds(pl.multiple_of(c * W + q * S, S), S)
            comb[:, columns] = term[q * T : (q + 1) * T]

    @pl.loop(0, G + 3)
    def _(c):
        @pl.when(c < G)
        def _():
            far_own(c)

        @pl.when(c == 0)
        def _():
            scatter_relay(near_s, 0)

        @pl.when((c >= 1) & (c <= G))
        def _():
            scatter_relay(far_s, c - 1)

        @pl.when(c == G)
        def _():
            scatter_own(near_s, 1)

        @pl.when(c < G - V)
        def _():
            near_outward(V + c)

        @pl.when(c == 2)
        def _():
            near_total(0)

        @pl.when(c >= 3)
        def _():
            far_total(c - 3)

        @pl.when(c == G + 2)
        def _():
            scatter_relay(near_s, 1)

        @pl.when(c >= 4)
        def _():
            far_combine(c - 4)

        @pl.when(c == G)
        def _():
            combine_near(0)

    near_total(1)
    far_combine(G - 1)
    combine_near(1)

    @pl.loop(0, G)
    def _(c):
        await_rows(far_disp, far_d_send, c, FAR)
        await_rows(far_back, far_b_send, c, FAR)
        for index in range(4):
            gather_hop(far_g, index, c).wait_send()
        for index in range(6):
            scatter_hop(far_s, index, c).wait_send()

    for u in range(U):
        await_rows(near_disp, near_d_send, u, V * B)
        await_rows(near_back, near_b_send, u, V * B)
        for index in range(6):
            near_hop(index, u).wait_send()
            scatter_hop(near_s, index, u).wait_send()


def fused(tokens, expert_ids, slot_ids, router, w_in, w_out):
    T, D = tokens.shape
    E = router.shape[1]
    C = 5 * T // (4 * E)
    H = w_in.shape[2]
    Q = 16 // math.gcd(16, C)
    G = min(CHUNKS, D // (128 * Q))
    U = 2
    W = D // G
    S = W // Q
    B, R = Q * C, E * C
    NEAR, FAR = 2 * (G // U) * B, (E - 2) * B
    NP, FP = -(-2 * C // 16) * 16, -(-(E - 2) * C // 16) * 16
    dims = (E, C, Q, G, U, W, S, T, H, NP, FP)
    vmem = pl.BlockSpec(memory_space=pltpu.VMEM)
    hbm = pl.BlockSpec(memory_space=pl.ANY)
    dma = pltpu.SemaphoreType.DMA
    rows = lambda near, far: [pltpu.VMEM((U, near, S), BF16), pltpu.VMEM((G, far, S), BF16)]
    return pl.pallas_call(
        functools.partial(kernel, dims),
        out_shape=pltpu.VMEM((T, D), BF16),
        in_specs=[hbm] * 6,
        out_specs=vmem,
        scratch_shapes=[
            pltpu.VMEM((T, D), BF16),
            pltpu.VMEM((1, T), jnp.int32),
            pltpu.VMEM((1, T), jnp.int32),
            pltpu.VMEM((E, D), BF16),
        ]
        + rows(NEAR, FAR)
        + rows(4 * NEAR, 4 * FAR)
        + [
            pltpu.VMEM((4 * NP, W), BF16),
            pltpu.VMEM((4 * FP, W), BF16),
            pltpu.VMEM((4 * NP, H), F32),
            pltpu.VMEM((4 * FP, H), F32),
            pltpu.VMEM((4 * NP, H), BF16),
            pltpu.VMEM((4 * FP, H), BF16),
            pltpu.VMEM((G, W, H), BF16),
            pltpu.VMEM((G, H, W), BF16),
        ]
        + rows(4 * NEAR, 4 * FAR)
        + rows(NEAR, FAR)
        + rows(2 * NEAR, 2 * FAR)
        + rows(NEAR, FAR)
        + rows(NEAR, FAR)
        + [
            pltpu.VMEM((E * B, Q * T), BF16),
            pltpu.VMEM((Q * NP, 2 * B), BF16),
            pltpu.VMEM((Q * FP, FAR), BF16),
            pltpu.VMEM((2 * B, Q * NP), BF16),
            pltpu.VMEM((FAR, Q * FP), BF16),
            pltpu.VMEM((Q * T, E * B), BF16),
            pltpu.VMEM((T, 1), F32),
            pltpu.VMEM((T, D), F32),
        ]
        + [dma((G,)), dma((G,)), dma((3,)), dma((U,))]
        + [dma((n,)) for n in (U, U, G, G)]
        + [dma((m, n)) for m, n in ((6, U), (6, U), (4, G), (4, G))]
        + [dma((6, n)) for n in (U, U, G, G)]
        + [dma((n,)) for n in (U, U, G, G)],
        compiler_params=pltpu.CompilerParams(
            collective_id=0, has_side_effects=True, vmem_limit_bytes=56 * 1024 * 1024
        ),
        cost_estimate=pl.CostEstimate(
            flops=16 * R * D * H, bytes_accessed=4 * D * H, transcendentals=T
        ),
    )(tokens, expert_ids.reshape(1, T), slot_ids.reshape(1, T), router.T, w_in, w_out)


def solution(mesh):
    body = fused if mesh.shape["section"] == 4 else per_device
    return jax.shard_map(
        body,
        mesh=mesh,
        in_specs=(
            P(("section", "expert"), None),
            P(("section", "expert")),
            P(("section", "expert")),
            P(),
            P("expert", None, "section"),
            P("expert", "section", None),
        ),
        out_specs=P(("section", "expert"), None),
        check_vma=False,
    )
```

```python
import functools
import math

import jax
import jax.numpy as jnp
from jax import lax
from jax.experimental import pallas as pl
from jax.experimental.pallas import tpu as pltpu
from jax.sharding import PartitionSpec as P

MESH = pl.DeviceIdType.MESH
BF16 = jnp.bfloat16
F32 = jnp.float32
CHUNKS = 8


def per_device(tokens, expert_ids, slot_ids, router, w_in, w_out):
    tok_rows, width_model = tokens.shape
    experts = router.shape[1]
    capacity = 5 * tok_rows // (4 * experts)
    cell_index = expert_ids * capacity + slot_ids
    onehot = (
        cell_index[None, :] == jnp.arange(experts * capacity, dtype=jnp.int32)[:, None]
    ).astype(jnp.bfloat16)
    dispatch = jnp.dot(onehot, tokens, preferred_element_type=jnp.float32).astype(jnp.bfloat16)
    dispatch = dispatch.reshape(experts, capacity, width_model)
    inward = w_in[0]
    outward = w_out[0]
    arrived = lax.all_to_all(dispatch, "expert", split_axis=0, concat_axis=0, tiled=True)
    flat = lax.all_gather(arrived.reshape(-1, width_model), "section", axis=0, tiled=True)
    hidden = jax.nn.relu(jnp.dot(flat, inward, preferred_element_type=jnp.float32)).astype(
        jnp.bfloat16
    )
    summed = lax.psum_scatter(
        jnp.dot(hidden, outward, preferred_element_type=jnp.float32).astype(jnp.bfloat16),
        "section",
        scatter_dimension=0,
        tiled=True,
    )
    expert_out = summed.reshape(experts, capacity, width_model)
    returned = lax.all_to_all(expert_out, "expert", split_axis=0, concat_axis=0, tiled=True)
    combined = lax.dot_general(
        onehot,
        returned.reshape(-1, width_model),
        (((0,), (0,)), ((), ())),
        preferred_element_type=jnp.float32,
    )
    logits = jnp.dot(tokens, router, preferred_element_type=jnp.float32)
    chosen = expert_ids[:, None] == jnp.arange(experts, dtype=jnp.int32)[None, :]
    gating = jax.nn.sigmoid(jnp.sum(jnp.where(chosen, logits, jnp.zeros_like(logits)), axis=1))
    return (gating[:, None] * combined).astype(jnp.bfloat16)


def divide(value, number):
    return lax.shift_right_logical(value * (-(-(1 << 20) // number)), 20)


def iota(shape, dim):
    return lax.broadcasted_iota(jnp.int32, shape, dim)


def one_where(condition):
    return jnp.where(condition, 1.0, 0.0).astype(BF16)


def dot(a, b):
    return jnp.dot(a, b, preferred_element_type=F32)


def kernel(
    dims, tok_hbm, eid_hbm, sid_hbm, router_hbm, w_in, w_out, out,
    tok, eid, sid, router,
    near_disp, far_disp, near_x, far_x, near_chunk, far_chunk, near_acc, far_acc, near_hid, far_hid, win, wout,
    near_part, far_part, near_half, far_half, near_fin, far_fin,
    near_back, far_back, near_ret, far_ret,
    d_mat, near_p, far_p, near_pt, far_pt, c_mat, gate, comb,
    win_sem, wout_sem, load_sem, tok_sem,
    near_d_send, near_d_recv, far_d_send, far_d_recv,
    near_g_send, near_g_recv, far_g_send, far_g_recv,
    near_s_send, near_s_recv, far_s_send, far_s_recv,
    near_b_send, near_b_recv, far_b_send, far_b_recv,
):
    E, C, Q, G, U, W, S, T, H, NP, FP = dims
    B, R = Q * C, E * C
    V = G // U
    NEAR, FAR = 2 * V * B, (E - 2) * B
    section, expert = lax.axis_index("section"), lax.axis_index("expert")
    y, x = section // 2, section % 2
    core = expert % 2
    chip = expert - core
    xn = {"section": y * 2 + (1 - x), "expert": expert}
    yn = {"section": (1 - y) * 2 + x, "expert": expert}
    sibling = {"section": section, "expert": chip + 1 - core}
    far = [({"section": section, "expert": (chip + d) % E}, d) for d in range(2, E)]

    def in_copy(c):
        return pltpu.make_async_copy(w_in.at[0, pl.ds(c * W, W)], win.at[c], win_sem.at[c])

    def out_copy(c):
        columns = pl.ds(pl.multiple_of(c * W, W), W)
        return pltpu.make_async_copy(w_out.at[0, :, columns], wout.at[c], wout_sem.at[c])

    def far_start(src, dst, send, recv, c):
        for target, d in far:
            row = pl.multiple_of((core + E - 2 * (d // 2) - 2) * B, 16)
            pltpu.make_async_remote_copy(
                src_ref=src.at[c, pl.ds((d - 2) * B, B)],
                dst_ref=dst.at[c, pl.ds(row, B)],
                send_sem=send.at[c],
                recv_sem=recv.at[c],
                device_id=target,
                device_id_type=MESH,
            ).start()

    def near_start(src, dst, send, recv, u):
        mine = pl.ds(pl.multiple_of(core * (V * B), 16), V * B)
        other = pl.ds(pl.multiple_of((1 - core) * (V * B), 16), V * B)
        pltpu.make_async_remote_copy(
            src_ref=src.at[u, other],
            dst_ref=dst.at[u, mine],
            send_sem=send.at[u],
            recv_sem=recv.at[u],
            device_id=sibling,
            device_id_type=MESH,
        ).start()
        pltpu.make_async_copy(src.at[u, mine], dst.at[u, mine], recv.at[u]).start()

    def await_rows(ref, sem, index, rows):
        view = ref.at[index, pl.ds(0, rows)]
        pltpu.make_async_copy(view, view, sem.at[index]).wait()

    def hop(src, src_row, dst, dst_row, rows, send, recv, index, c, target):
        return pltpu.make_async_remote_copy(
            src_ref=src.at[c, pl.ds(src_row, rows)],
            dst_ref=dst.at[c, pl.ds(dst_row, rows)],
            send_sem=send.at[index, c],
            recv_sem=recv.at[index, c],
            device_id=target,
            device_id_type=MESH,
        )

    def gather_hop(buffers, index, c):
        held, n, send, recv = buffers
        h = n // 2
        src_row, dst_row, rows, target = (
            (0, n, n, xn),
            (0, 2 * n, n, yn),
            (n, 3 * n, h, yn),
            (2 * n + h, 3 * n + h, h, xn),
        )[index]
        return hop(held, src_row, held, dst_row, rows, send, recv, index, c, target)

    def near_hop(index, u):
        own = pl.multiple_of(core * (V * B), 16)
        other = pl.multiple_of((1 - core) * (V * B), 16)
        src, src_row, target, base = (
            (near_disp, own, xn, NEAR),
            (near_disp, own, yn, 2 * NEAR),
            (near_x, other, xn, NEAR),
            (near_x, other, yn, 2 * NEAR),
            (near_x, NEAR, yn, 3 * NEAR),
            (near_x, 2 * NEAR + V * B, xn, 3 * NEAR + V * B),
        )[index]
        dst_row = base if index >= 4 else base + src_row
        if index < 4:
            dst_row = pl.multiple_of(dst_row, 16)
        return hop(
            src, src_row, near_x, dst_row, V * B, near_g_send, near_g_recv, index, u, target
        )

    def scatter_hop(buffers, index, c):
        part, half, fin, n, send, recv = buffers
        h = n // 2
        src_row, dst, dst_row, target = (
            (3 * n, half, 0, xn),
            (3 * n + h, half, h, yn),
            (n, fin, 0, xn),
            (2 * n + h, fin, n + h, yn),
            (n + h, fin, h, xn),
            (2 * n, fin, n, yn),
        )[index]
        return hop(part, src_row, dst, dst_row, h, send, recv, index, c, target)

    far_g = (far_x, FAR, far_g_send, far_g_recv)
    near_s = (near_part, near_half, near_fin, NEAR, near_s_send, near_s_recv)
    far_s = (far_part, far_half, far_fin, FAR, far_s_send, far_s_recv)

    def gather_own(buffers, c):
        gather_hop(buffers, 0, c).start()
        gather_hop(buffers, 1, c).start()

    def gather_relay(buffers, c):
        gather_hop(buffers, 0, c).wait_recv()
        gather_hop(buffers, 2, c).start()
        gather_hop(buffers, 1, c).wait_recv()
        gather_hop(buffers, 3, c).start()

    def gather_rest(buffers, c):
        gather_hop(buffers, 2, c).wait_recv()
        gather_hop(buffers, 3, c).wait_recv()

    def scatter_own(buffers, c):
        for index in range(4):
            scatter_hop(buffers, index, c).start()

    def scatter_relay(buffers, c):
        part, half, _, n, _, _ = buffers
        h = n // 2
        for wait, row, at, send in ((0, 2 * n, 0, 5), (1, n + h, h, 4)):
            scatter_hop(buffers, wait, c).wait_recv()
            part[c, row : row + h] = (
                part[c, row : row + h].astype(F32) + half[c, at : at + h].astype(F32)
            ).astype(BF16)
            scatter_hop(buffers, send, c).start()

    def scatter_total(buffers, c, back):
        part, _, fin, n, _, _ = buffers
        for index in range(2, 6):
            scatter_hop(buffers, index, c).wait_recv()
        back[c] = (
            part[c, 0:n].astype(F32) + fin[c, 0:n].astype(F32) + fin[c, n : 2 * n].astype(F32)
        ).astype(BF16)

    barrier = pltpu.get_barrier_semaphore()
    for target in [target for target, _ in far] + [sibling, xn, yn]:
        pl.semaphore_signal(barrier, inc=1, device_id=target, device_id_type=MESH)

    loads = [
        pltpu.make_async_copy(src, dst, load_sem.at[i])
        for i, (src, dst) in enumerate(((eid_hbm, eid), (sid_hbm, sid), (router_hbm, router)))
    ]
    halves = [slice(u * V * W, (u + 1) * V * W) for u in range(U)]
    tok_loads = [
        pltpu.make_async_copy(tok_hbm.at[:, part], tok.at[:, part], tok_sem.at[u])
        for u, part in enumerate(halves)
    ]
    for copy in loads[0:2] + tok_loads + loads[2:]:
        copy.start()
    loads[0].wait()
    loads[1].wait()

    def keys(shape, dim, first, stride):
        r = iota(shape, dim)
        block = divide(r, B)
        inner = r - block * B
        quarter = divide(inner, C)
        owner = block + first
        owner = jnp.where(owner >= E, owner - E, owner)
        return quarter * stride + owner * C + (inner - quarter * C)

    cell_row = eid[...] * C + sid[...]
    diagonal = iota((T, T), 0) == iota((T, T), 1)

    def column(row):
        spread = jnp.where(diagonal, jnp.broadcast_to(row, (T, T)), 0).astype(F32)
        return jnp.sum(spread, axis=1, keepdims=True).astype(jnp.int32)

    key = keys((E * B, T), 0, chip, R)
    for q in range(Q):
        d_mat[:, q * T : (q + 1) * T] = one_where(key == cell_row + q * R)

    def stacked(c):
        return jnp.concatenate(
            [tok[:, pl.ds(pl.multiple_of(c * W + q * S, S), S)] for q in range(Q)], axis=0
        )

    def far_dispatch(c):
        far_disp[c] = dot(d_mat[2 * B :], stacked(c)).astype(BF16)
        far_start(far_disp, far_x, far_d_send, far_d_recv, c)

    def near_dispatch(u):
        tok_loads[u].wait()
        for v in range(V):
            rows = dot(d_mat[0 : 2 * B], stacked(u * V + v)).astype(BF16)
            near_disp[u, v * B : (v + 1) * B] = rows[0:B]
            near_disp[u, (V + v) * B : (V + v + 1) * B] = rows[B : 2 * B]

    def near_begin(u):
        near_start(near_disp, near_x, near_d_send, near_d_recv, u)
        near_hop(0, u).start()
        near_hop(1, u).start()

    near_dispatch(0)
    pl.semaphore_wait(barrier, E + 1)
    near_begin(0)
    for u in range(1, U):
        near_dispatch(u)
        near_begin(u)
    for u in range(U):
        await_rows(near_x, near_d_recv, u, NEAR)
        near_hop(2, u).start()
        near_hop(3, u).start()
        far_dispatch(u)

    @pl.loop(0, G)
    def _(c):
        in_copy(c).start()

    def order(p, pt, rows, stride):
        p[...] = one_where(keys((Q * stride, rows), 1, 0, stride) == iota((Q * stride, rows), 0))
        pt[...] = one_where(keys((rows, Q * stride), 0, 0, stride) == iota((rows, Q * stride), 1))

    order(near_p, near_pt, 2 * B, NP)
    order(far_p, far_pt, FAR, FP)
    near_acc[...] = jnp.zeros_like(near_acc)
    far_acc[...] = jnp.zeros_like(far_acc)

    def widen(raw, p, chunk, stride):
        moved = dot(p[...], jnp.concatenate(raw, axis=1)).astype(BF16)
        for s in range(4):
            for q in range(Q):
                chunk[s * stride : (s + 1) * stride, q * S : (q + 1) * S] = moved[
                    q * stride : (q + 1) * stride, s * S : (s + 1) * S
                ]

    def narrow(chunk, pt, stride):
        rows = [
            jnp.concatenate(
                [chunk[s * stride : (s + 1) * stride, q * S : (q + 1) * S] for s in range(4)],
                axis=1,
            )
            for q in range(Q)
        ]
        return dot(pt[...], jnp.concatenate(rows, axis=0)).astype(BF16)

    def inward(acc, chunk, k):
        @pl.loop(0, H // 256, unroll=True)
        def _(n):
            columns = pl.ds(pl.multiple_of(n * 256, 256), 256)
            acc[:, columns] += dot(chunk[...], win[k, :, columns])

    def activate(acc, hid):
        @pl.loop(0, H // 256, unroll=True)
        def _(n):
            columns = pl.ds(pl.multiple_of(n * 256, 256), 256)
            hid[:, columns] = jnp.maximum(acc[:, columns], 0.0).astype(BF16)

    def outward(hid, chunk, k):
        @pl.loop(0, W // 256, unroll=True)
        def _(n):
            columns = pl.ds(pl.multiple_of(n * 256, 256), 256)
            chunk[:, columns] = dot(hid[...], wout[k, :, columns]).astype(BF16)

    def near_inward(k):
        raw = [jnp.concatenate(near_rows(near_x, k, s * NEAR), axis=0) for s in range(4)]
        widen(raw, near_p, near_chunk, NP)
        in_copy(k).wait()
        inward(near_acc, near_chunk, k)

    def near_outward(k):
        out_copy(k).wait()
        outward(near_hid, near_chunk, k)
        moved = narrow(near_chunk, near_pt, NP)
        u, v = k // V, k % V
        for s in range(4):
            columns = slice(s * S, (s + 1) * S)
            first = pl.multiple_of(s * NEAR + v * B, 16)
            second = pl.multiple_of(s * NEAR + (V + v) * B, 16)
            near_part[u, pl.ds(first, B)] = moved[0:B, columns]
            near_part[u, pl.ds(second, B)] = moved[B : 2 * B, columns]

    def near_rows(ref, k, base):
        u, v = k // V, k % V
        first = pl.multiple_of(base + v * B, 16)
        second = pl.multiple_of(base + (V + v) * B, 16)
        return [ref[u, pl.ds(first, B)], ref[u, pl.ds(second, B)]]

    @pl.loop(0, G + 4)
    def _(c):
        @pl.when(c + 2 < G)
        def _():
            far_dispatch(c + 2)

        @pl.when(c < G)
        def _():
            out_copy(c).start()
            await_rows(far_x, far_d_recv, c, FAR)
            gather_own(far_g, c)

        @pl.when(c < U)
        def _():
            near_hop(0, c).wait_recv()
            near_hop(2, c).wait_recv()
            near_hop(4, c).start()
            near_hop(1, c).wait_recv()
            near_hop(3, c).wait_recv()
            near_hop(5, c).start()

        @pl.when(c == 0)
        def _():
            key = keys((T, E * B), 1, chip, R)
            cell_column = column(cell_row)
            for q in range(Q):
                c_mat[q * T : (q + 1) * T] = one_where(key == cell_column + q * R)
            loads[2].wait()
            logits = lax.dot_general(
                tok[...], router[...], (((1,), (1,)), ((), ())), preferred_element_type=F32
            )
            chosen = column(eid[...]) == iota((T, E), 1)
            picked = jnp.sum(jnp.where(chosen, logits, 0.0), axis=1, keepdims=True)
            gate[...] = 1.0 / (1.0 + jnp.exp(-picked))

        @pl.when((c >= 2) & (c < G + 2))
        def _():
            gather_relay(far_g, c - 2)

        @pl.when(c == 3)
        def _():
            for u in range(U):
                near_hop(4, u).wait_recv()
                near_hop(5, u).wait_recv()

        @pl.when((c >= 4) & (c < 4 + G // 2))
        def _():
            for i in range(2):
                near_inward(2 * (c - 4) + i)

        @pl.when(c == 4 + G // 2)
        def _():
            activate(near_acc, near_hid)

        @pl.when((c >= 4 + G // 2) & (c < 4 + G // 2 + V // 2))
        def _():
            for i in range(2):
                near_outward(2 * (c - 4 - G // 2) + i)

        @pl.when(c == 3 + G // 2 + V // 2)
        def _():
            scatter_own(near_s, 0)

        @pl.when(c >= 4)
        def _():
            k = c - 4
            gather_rest(far_g, k)
            widen([far_x[k, s * FAR : (s + 1) * FAR] for s in range(4)], far_p, far_chunk, FP)
            inward(far_acc, far_chunk, k)

    activate(far_acc, far_hid)

    def combine_near(u):
        await_rows(near_ret, near_b_recv, u, NEAR)
        for v in range(V):
            rows = jnp.concatenate(near_rows(near_ret, u * V + v, 0), axis=0)
            term = dot(c_mat[:, 0 : 2 * B], rows)
            for q in range(Q):
                at = (u * V + v) * W + q * S
                out[:, at : at + S] = (
                    gate[...] * (comb[:, at : at + S] + term[q * T : (q + 1) * T])
                ).astype(BF16)

    def far_own(c):
        outward(far_hid, far_chunk, c)
        moved = narrow(far_chunk, far_pt, FP)
        for s in range(4):
            far_part[c, s * FAR : (s + 1) * FAR] = moved[:, s * S : (s + 1) * S]
        scatter_own(far_s, c)

    def far_total(c):
        scatter_total(far_s, c, far_back)
        far_start(far_back, far_ret, far_b_send, far_b_recv, c)

    def near_total(u):
        scatter_total(near_s, u, near_back)
        near_start(near_back, near_ret, near_b_send, near_b_recv, u)

    def far_combine(c):
        await_rows(far_ret, far_b_recv, c, FAR)
        term = dot(c_mat[:, 2 * B :], far_ret[c])
        for q in range(Q):
            columns = pl.ds(pl.multiple_of(c * W + q * S, S), S)
            comb[:, columns] = term[q * T : (q + 1) * T]

    @pl.loop(0, G + 3)
    def _(c):
        @pl.when(c < G)
        def _():
            far_own(c)

        @pl.when(c == 0)
        def _():
            scatter_relay(near_s, 0)

        @pl.when((c >= 1) & (c <= G))
        def _():
            scatter_relay(far_s, c - 1)

        @pl.when(c == G)
        def _():
            scatter_own(near_s, 1)

        @pl.when(c < G - V)
        def _():
            near_outward(V + c)

        @pl.when(c == 2)
        def _():
            near_total(0)

        @pl.when(c >= 3)
        def _():
            far_total(c - 3)

        @pl.when(c == G + 2)
        def _():
            scatter_relay(near_s, 1)

        @pl.when(c >= 4)
        def _():
            far_combine(c - 4)

        @pl.when(c == G)
        def _():
            combine_near(0)

    near_total(1)
    far_combine(G - 1)
    combine_near(1)

    @pl.loop(0, G)
    def _(c):
        await_rows(far_disp, far_d_send, c, FAR)
        await_rows(far_back, far_b_send, c, FAR)
        for index in range(4):
            gather_hop(far_g, index, c).wait_send()
        for index in range(6):
            scatter_hop(far_s, index, c).wait_send()

    for u in range(U):
        await_rows(near_disp, near_d_send, u, V * B)
        await_rows(near_back, near_b_send, u, V * B)
        for index in range(6):
            near_hop(index, u).wait_send()
            scatter_hop(near_s, index, u).wait_send()


def fused(tokens, expert_ids, slot_ids, router, w_in, w_out):
    T, D = tokens.shape
    E = router.shape[1]
    C = 5 * T // (4 * E)
    H = w_in.shape[2]
    Q = 16 // math.gcd(16, C)
    G = min(CHUNKS, D // (128 * Q))
    U = 2
    W = D // G
    S = W // Q
    B, R = Q * C, E * C
    NEAR, FAR = 2 * (G // U) * B, (E - 2) * B
    NP, FP = -(-2 * C // 16) * 16, -(-(E - 2) * C // 16) * 16
    dims = (E, C, Q, G, U, W, S, T, H, NP, FP)
    vmem = pl.BlockSpec(memory_space=pltpu.VMEM)
    hbm = pl.BlockSpec(memory_space=pl.ANY)
    dma = pltpu.SemaphoreType.DMA
    rows = lambda near, far: [pltpu.VMEM((U, near, S), BF16), pltpu.VMEM((G, far, S), BF16)]
    return pl.pallas_call(
        functools.partial(kernel, dims),
        out_shape=pltpu.VMEM((T, D), BF16),
        in_specs=[hbm] * 6,
        out_specs=vmem,
        scratch_shapes=[
            pltpu.VMEM((T, D), BF16),
            pltpu.VMEM((1, T), jnp.int32),
            pltpu.VMEM((1, T), jnp.int32),
            pltpu.VMEM((E, D), BF16),
        ]
        + rows(NEAR, FAR)
        + rows(4 * NEAR, 4 * FAR)
        + [
            pltpu.VMEM((4 * NP, W), BF16),
            pltpu.VMEM((4 * FP, W), BF16),
            pltpu.VMEM((4 * NP, H), F32),
            pltpu.VMEM((4 * FP, H), F32),
            pltpu.VMEM((4 * NP, H), BF16),
            pltpu.VMEM((4 * FP, H), BF16),
            pltpu.VMEM((G, W, H), BF16),
            pltpu.VMEM((G, H, W), BF16),
        ]
        + rows(4 * NEAR, 4 * FAR)
        + rows(NEAR, FAR)
        + rows(2 * NEAR, 2 * FAR)
        + rows(NEAR, FAR)
        + rows(NEAR, FAR)
        + [
            pltpu.VMEM((E * B, Q * T), BF16),
            pltpu.VMEM((Q * NP, 2 * B), BF16),
            pltpu.VMEM((Q * FP, FAR), BF16),
            pltpu.VMEM((2 * B, Q * NP), BF16),
            pltpu.VMEM((FAR, Q * FP), BF16),
            pltpu.VMEM((Q * T, E * B), BF16),
            pltpu.VMEM((T, 1), F32),
            pltpu.VMEM((T, D), F32),
        ]
        + [dma((G,)), dma((G,)), dma((3,)), dma((U,))]
        + [dma((n,)) for n in (U, U, G, G)]
        + [dma((m, n)) for m, n in ((6, U), (6, U), (4, G), (4, G))]
        + [dma((6, n)) for n in (U, U, G, G)]
        + [dma((n,)) for n in (U, U, G, G)],
        compiler_params=pltpu.CompilerParams(
            collective_id=0, has_side_effects=True, vmem_limit_bytes=56 * 1024 * 1024
        ),
        cost_estimate=pl.CostEstimate(
            flops=16 * R * D * H, bytes_accessed=4 * D * H, transcendentals=T
        ),
    )(tokens, expert_ids.reshape(1, T), slot_ids.reshape(1, T), router.T, w_in, w_out)


def solution(mesh):
    body = fused if mesh.shape["section"] == 4 else per_device
    return jax.shard_map(
        body,
        mesh=mesh,
        in_specs=(
            P(("section", "expert"), None),
            P(("section", "expert")),
            P(("section", "expert")),
            P(),
            P("expert", None, "section"),
            P("expert", "section", None),
        ),
        out_specs=P(("section", "expert"), None),
        check_vma=False,
    )
```
